256 devices in a mesh: dp: 4 (over x), graph: 64 (over z, y, core).
Axes of the slice: x: 4, y: 4, z: 8, core: 2. Of those that a mesh axis runs over, the one named last changes fastest.
Arguments:
- tokens: bfloat16 [8192, 32, 768], P(('dp', 'graph'))
- w_in: bfloat16 [768, 3072], replicated, may hold values from -0.21875 to 0.21875
- w_out: bfloat16 [3072, 768], replicated, may hold values from -0.109375 to 0.109375
- tile_weights: bfloat16 [8192, 128, 128], P(('dp', 'graph')), may hold values from 0 to 18, as said below
- tile_src: int32 [8192], P(('dp', 'graph')), may hold values from 0 to 15
- tile_dst: int32 [8192], P(('dp', 'graph')), may hold values from 0 to 15, as said below
- w_sage: bfloat16 [1536, 1024], P(None, 'dp'), may hold values from -0.15625 to 0.15625
Outputs:
- embeddings: bfloat16 [8192, 768], P(('dp', 'graph'))
- node_states: bfloat16 [8192, 1024], P(('dp', 'graph'))
The draws below stay inside these ranges and needn't reach their ends.
Inputs may be any that keep to these rules, and one draw needn't show every extreme that they name: `tile_weights`: zero where a tile has no edge, positive on an edge. `tile_dst`: among the 32 tiles of one device no destination block appears more than 4 times; in every slab one block, drawn from the seed, is the destination of exactly 4 tiles of every device of the slab.
All inputs are finite; a program needn't handle non-finite values.
Results may differ from the reference program's by a relative error of at most 0.0042.
The reference program's roundings to bfloat16 on the way (of `hidden` and `aggregated`) count: a program that leaves them out, or rounds other values in their place, can miss the bound.
Values may be sent and summed in bfloat16 or wider, within the bound.
A program may use at most 128 MiB of HBM per device.

```python
import math
import jax
import jax.numpy as jnp
from jax import lax

D = 768
FF = 3072
HID = 1024
BLK = 128
TOK_ABS = 32
NODE_DEV = 32
TILES_DEV = 32
NODES = 8192
GROUP_NODES = 2048
BLOCKS = 16
TILES = 8192
GROUP_TILES = 2048
CAPB = 4
N_GRAPH = 64
DEVICES = 256


def draw_tokens(key, part):
    base_draw = jax.random.normal(jax.random.fold_in(key, 1), (NODES, TOK_ABS, D), jnp.float32)
    return base_draw.astype(jnp.bfloat16)


def draw_tile_weights(key, part):
    row_share = jnp.exp(jax.random.uniform(jax.random.fold_in(key, 1), (TILES, BLK, 1), jnp.float32, math.log(0.1), 0.0))
    present = jax.random.uniform(jax.random.fold_in(key, 2), (TILES, BLK, BLK), jnp.float32) < row_share
    device_place = jnp.arange(TILES) // TILES_DEV % N_GRAPH
    position = device_place.astype(jnp.float32) / max(N_GRAPH - 1, 1)
    rising = 1.0 + 2.0 * position
    edge_value = jax.random.uniform(jax.random.fold_in(key, 3), (TILES, BLK, BLK), jnp.float32, 0.5, 1.5)
    return jnp.where(present, edge_value * rising[:, None, None], 0.0).astype(jnp.bfloat16)


def draw_tile_dst(key, part):
    slab_total = DEVICES // N_GRAPH
    hub_blocks = jax.random.randint(jax.random.fold_in(key, 11), (slab_total,), 0, BLOCKS)
    device_hubs = jnp.repeat(hub_blocks, N_GRAPH)
    device_keys = jax.random.split(jax.random.fold_in(key, 12), DEVICES)

    def one_device(device_key, hub_block):
        pool = jnp.arange(BLOCKS * CAPB, dtype=jnp.int32) // CAPB
        shuffled = jax.random.permutation(jax.random.fold_in(device_key, 1), pool)
        order = jnp.argsort((shuffled == hub_block).astype(jnp.int32), stable=True)
        others = shuffled[order][:TILES_DEV - CAPB]
        slots = jnp.concatenate([jnp.zeros((CAPB,), jnp.int32) + hub_block, others])
        return jax.random.permutation(jax.random.fold_in(device_key, 2), slots)
    return jax.vmap(one_device)(device_keys, device_hubs).reshape(TILES).astype(jnp.int32)


def plant(array, rng, low, top_value):
    longest = array.shape.index(max(array.shape))
    spots = []
    for shift in (0, 1):
        where = [jax.random.randint(jax.random.fold_in(rng, axis), (), 0, length) for axis, length in enumerate(array.shape)]
        where[longest] = (where[longest] + shift) % array.shape[longest]
        spots.append(tuple(where))
    return array.at[spots[0]].set(low).at[spots[1]].set(top_value)


def block_levels(rng, dims, shards, least, top_value):
    def one(dim, parts):
        draws = jax.random.uniform(jax.random.fold_in(jax.random.fold_in(rng, 6), dim), (parts,), jnp.float32, least / len(shards), top_value / len(shards))
        return jnp.repeat(jnp.exp(draws), dims[dim] // parts).reshape((-1,) + (1,) * (len(dims) - dim - 1))

    gain = one(*shards[0])
    for cut in shards[1:]:
        gain = gain * one(*cut)
    return gain


def bell_draw(stream_key, extent, scale, bound, cuts=(), kind=jnp.bfloat16):
    factor_of = block_levels(stream_key, extent, cuts, -0.22, 0.18) if cuts else 1.0
    drawn = jax.random.normal(stream_key, extent, jnp.float32) * scale * factor_of
    return jnp.minimum(jnp.maximum(drawn, -bound), bound).astype(kind)


def setup_inputs(seed: int = 0) -> dict:
    key_list = jax.random.split(jax.random.key(seed), 8)
    tokens = draw_tokens(jax.random.fold_in(key_list[7], 71), 0)
    w_in = bell_draw(key_list[1], (D, FF), D ** -0.5, 0.21875)
    w_out = bell_draw(key_list[2], (FF, D), FF ** -0.5, 0.109375)
    tile_weights = draw_tile_weights(jax.random.fold_in(key_list[7], 71), 0)
    tile_src = plant(jax.random.randint(key_list[4], (TILES,), 0, BLOCKS), jax.random.fold_in(key_list[4], 1), 0, BLOCKS - 1).astype(jnp.int32)
    tile_dst = draw_tile_dst(jax.random.fold_in(key_list[7], 71), 0)
    w_sage = bell_draw(key_list[6], (2 * D, HID), (2 * D) ** -0.5, 0.15625, ((1, 4),))
    return dict(tokens=tokens, w_in=w_in, w_out=w_out, tile_weights=tile_weights, tile_src=tile_src, tile_dst=tile_dst, w_sage=w_sage)


EPS = 1e-05

def encode(block_tokens, w_in, w_out):
    node_total, token_total, feature_width = block_tokens.shape
    flat = block_tokens.reshape(node_total * token_total, feature_width)
    hidden = jax.nn.gelu(jnp.dot(flat, w_in, preferred_element_type=jnp.float32), approximate=False).astype(jnp.bfloat16)
    mixed = flat.astype(jnp.float32) + jnp.dot(hidden, w_out, preferred_element_type=jnp.float32)
    center = mixed - lax.optimization_barrier(jnp.mean(mixed, axis=1, keepdims=True))
    normed = center * lax.rsqrt(lax.optimization_barrier(jnp.mean(center * center, axis=1, keepdims=True)) + EPS)
    return lax.optimization_barrier(jnp.mean(normed.reshape(node_total, token_total, feature_width), axis=1)).astype(jnp.bfloat16)

def reference(tokens, w_in, w_out, tile_weights, tile_src, tile_dst, w_sage):
    feature_width = tokens.shape[2]
    per_device = tokens.reshape(DEVICES, NODE_DEV, TOK_ABS, feature_width)
    embedded = lax.map(lambda block_tokens: encode(block_tokens, w_in, w_out), per_device)
    embedded = embedded.reshape(NODES, feature_width)
    slabs = NODES // GROUP_NODES

    def one_slab(inputs):
        slab_emb, slab_tiles, slab_src, slab_dst = inputs
        adjacency = jnp.zeros((BLOCKS, BLK, BLOCKS, BLK), jnp.float32)
        adjacency = adjacency.at[slab_dst.astype(jnp.int32), :, slab_src.astype(jnp.int32), :].add(slab_tiles.astype(jnp.float32))
        adjacency = adjacency.reshape(GROUP_NODES, GROUP_NODES)
        neighbor_sums = jnp.dot(adjacency, slab_emb.astype(jnp.float32), precision=lax.Precision.HIGHEST)
        degree = lax.optimization_barrier(jnp.sum(adjacency, axis=1))
        aggregated = (neighbor_sums * lax.rsqrt(1.0 + degree)[:, None]).astype(jnp.bfloat16)
        joined = jnp.concatenate([slab_emb, aggregated], axis=1)
        preact = jnp.dot(joined, w_sage, preferred_element_type=jnp.float32)
        activated = jnp.maximum(preact, 0.0)
        node_out = activated * lax.rsqrt(lax.optimization_barrier(jnp.mean(activated * activated, axis=1, keepdims=True)) + EPS)
        return node_out.astype(jnp.bfloat16)
    states = lax.map(one_slab, (embedded.reshape(slabs, GROUP_NODES, feature_width), tile_weights.reshape(slabs, GROUP_TILES, BLK, BLK), tile_src.reshape(slabs, GROUP_TILES), tile_dst.reshape(slabs, GROUP_TILES)))
    return (embedded, states.reshape(NODES, HID))
```

```python
import functools

import jax
import jax.numpy as jnp
from jax import lax
from jax.experimental import pallas as pl
from jax.experimental.pallas import tpu as pltpu
from jax.sharding import PartitionSpec as P

EPS = 1e-05
MESH = pl.DeviceIdType.MESH

NX, NZ, NY, NC = 4, 8, 4, 2
D, FF, HID = 768, 3072, 1024
BLK, TILES, BLOCKS = 128, 32, 16
NODES, TOK = 32, 32
CHUNKS = 4
CN = NODES // CHUNKS
ROWS = CN * TOK
FB = 768
NFB = FF // FB
QUAD = 4
SUB = BLK // QUAD
FC = 256
NFC = D // FC
BF, F32 = jnp.bfloat16, jnp.float32


def kernel(
    tok_ref, win_ref, wout_ref, tw_ref, src_ref, dst_ref, ws_ref,
    emb_out, node_out,
    win, wout, tok, tiles, ids, spread, adj, emb, wg, own, out_y, in_y, out_z, in_z,
    deg, deg_in, deg_sum, deg_all,
    load_sem, tile_s, tile_r, id_s, id_r, w_s, w_r, z_s, z_r, y_s, y_r, c_s, c_r,
    vy_s, vy_r, vz_s, vz_r, d_s, d_r,
):
    xi = lax.axis_index("dp")
    g = lax.axis_index("graph")
    z, y, c = g // 8, (g // 2) % 4, g % 2
    q = g % 4
    yh = y // 2

    def at(zz, yy, cc):
        return (xi, (zz * NY + yy) * NC + cc)

    def zoff(j):
        return lax.rem(z + j + NZ, NZ)

    def yoff(j):
        return lax.rem(y + j + NY, NY)

    def xoff(j):
        return lax.rem(xi + j + NX, NX)

    def remote(src, dst, ss, rs, dev):
        return pltpu.make_async_remote_copy(
            src_ref=src, dst_ref=dst, send_sem=ss, recv_sem=rs, device_id=dev, device_id_type=MESH
        )

    sib = at(z, y, 1 - c)
    def load_tok(k):
        return pltpu.make_async_copy(tok_ref.at[pl.ds(k * CN, CN)], tok.at[pl.ds(k * CN, CN)], load_sem.at[k])

    def load_in(j):
        cols = pl.ds(j * FB, FB)
        return pltpu.make_async_copy(win_ref.at[:, cols], win.at[:, cols], load_sem.at[4 + j])

    def load_out(j):
        rows = pl.ds(j * FB, FB)
        return pltpu.make_async_copy(wout_ref.at[rows], wout.at[rows], load_sem.at[8 + j])

    def load_tiles():
        return pltpu.make_async_copy(
            tw_ref.at[:, pl.ds(pl.multiple_of(q * SUB, SUB), SUB)], tiles.at[q], load_sem.at[12]
        )

    def load_ws(h):
        return pltpu.make_async_copy(ws_ref.at[pl.ds(h * D, D)], wg.at[h, xi], load_sem.at[13 + h])

    peers = [at(zoff(j), y, c) for j in range(1, NZ)]
    peers += [at(z, yoff(j), c) for j in range(1, NY)]
    ypair = y + 1 - 2 * (y % 2)
    peers += [sib, at(z, ypair, 1 - c), (xoff(1), g), (xoff(-1), g)]
    barrier = pltpu.get_barrier_semaphore()
    for dev in peers:
        pl.semaphore_signal(barrier, inc=1, device_id=dev, device_id_type=MESH)

    load_tok(0).start()
    for j in range(NFB):
        load_in(j).start()
        load_out(j).start()
    for k in range(1, CHUNKS):
        load_tok(k).start()
    load_tiles().start()
    for h in range(2):
        load_ws(h).start()

    lane = lax.broadcasted_iota(jnp.int32, (8, 128), 1) - q * TILES
    mine = jnp.full((8, 128), -1, jnp.int32)
    for t in range(TILES):
        mine = jnp.where(lane == t, src_ref[t] * BLOCKS + dst_ref[t], mine)
    ids[q] = mine

    pl.semaphore_wait(barrier, len(peers))

    quad = [(at(z, y, 1 - c), q + 1 - 2 * (q % 2)), (at(z, ypair, c), lax.rem(q + 2, 4)),
            (at(z, ypair, 1 - c), lax.rem(q + 2, 4) + 1 - 2 * (q % 2))]

    def tile_send(n):
        dev, dq = quad[n]
        return remote(tw_ref.at[:, pl.ds(pl.multiple_of(dq * SUB, SUB), SUB)], tiles.at[q],
                      tile_s.at[n], tile_r.at[n], dev)

    def tile_recv(n):
        dev, dq = quad[n]
        return remote(tiles.at[dq], tiles.at[dq], tile_s.at[n], tile_r.at[n], dev)

    def id_send(n):
        return remote(ids.at[q], ids.at[q], id_s.at[n], id_r.at[n], quad[n][0])

    def id_recv(n):
        dq = quad[n][1]
        return remote(ids.at[dq], ids.at[dq], id_s.at[n], id_r.at[n], quad[n][0])

    for n in range(3):
        id_send(n).start()
        tile_send(n).start()

    half = pl.ds(pl.multiple_of(c * D, D), D)

    def w_send(n):
        return remote(ws_ref.at[half], wg.at[c, xi], w_s.at[n], w_r.at[n], (xoff(1 - 2 * n), g))

    def w_recv(n):
        slot = wg.at[c, xoff(2 * n - 1)]
        return remote(slot, slot, w_s.at[n], w_r.at[n], (xoff(1 - 2 * n), g))

    def w_fwd(n):
        rows = pl.ds(n * (D // 2), D // 2)
        slot = wg.at[c, xoff(2 * n - 1), rows]
        return remote(slot, slot, w_s.at[2 + n], w_r.at[2 + n], (xoff(1 - 2 * n), g))

    def w_fwd_recv(n):
        rows = pl.ds(n * (D // 2), D // 2)
        slot = wg.at[c, xoff(2), rows]
        return remote(slot, slot, w_s.at[2 + n], w_r.at[2 + n], (xoff(1 - 2 * n), g))

    def w_sib(n):
        slot = wg.at[c, xoff(n)]
        return remote(slot, slot, w_s.at[3 + n], w_r.at[3 + n], sib)

    def w_sib_recv(n):
        slot = wg.at[1 - c, xoff(n)]
        return remote(slot, slot, w_s.at[3 + n], w_r.at[3 + n], sib)

    for n in range(2):
        w_send(n).start()

    def z_send(k, j):
        slot = emb.at[z, y, c, k]
        return remote(slot, slot, z_s.at[k, j], z_r.at[k, j], at(zoff(j), y, c))

    def z_recv(k, j):
        slot = emb.at[zoff(-j), y, c, k]
        return remote(slot, slot, z_s.at[k, j], z_r.at[k, j], at(zoff(j), y, c))

    def y_send(k, j):
        slot = emb.at[:, y, c, k]
        return remote(slot, slot, y_s.at[k, j], y_r.at[k, j], at(z, yoff(j), c))

    def y_recv(k, j):
        slot = emb.at[:, yoff(-j), c, k]
        return remote(slot, slot, y_s.at[k, j], y_r.at[k, j], at(z, yoff(j), c))

    def c_send(k):
        slot = emb.at[:, :, c, k]
        return remote(slot, slot, c_s.at[k], c_r.at[k], sib)

    def c_recv(k):
        slot = emb.at[:, :, 1 - c, k]
        return remote(slot, slot, c_s.at[k], c_r.at[k], sib)

    def go_z(k):
        for j in (4, 3, 5, 2, 6, 1, 7):
            z_send(k, j).start()

    def go_y(k):
        for j in range(1, NZ):
            z_recv(k, j).wait_recv()
        for j in (2, 1, 3):
            y_send(k, j).start()

    def go_c(k):
        for j in range(1, NY):
            y_recv(k, j).wait_recv()
        c_send(k).start()

    def encode(k, carry):
        load_tok(k).wait()
        x = tok[pl.ds(k * CN, CN)].reshape(ROWS, D)
        acc = x.astype(F32)
        for j in range(NFB):
            @pl.when(k == 0)
            def _():
                load_in(j).wait()
                load_out(j).wait()

            h = jnp.dot(x, win[:, j * FB:(j + 1) * FB], preferred_element_type=F32)
            a = (h * 0.5 * (1.0 + lax.erf(h * 0.7071067811865476))).astype(BF)
            acc = acc + jnp.dot(a, wout[j * FB:(j + 1) * FB, :], preferred_element_type=F32)
            if j == 1:
                @pl.when(k >= 2)
                def _():
                    go_y(k - 2)

                @pl.when(k == 3)
                def _():
                    go_c(0)
                    for n in range(2):
                        w_recv(n).wait_recv()
                        w_fwd(n).start()
        cent = acc - jnp.mean(acc, axis=1, keepdims=True)
        var = jnp.mean(cent * cent, axis=1, keepdims=True)
        norm = cent * lax.rsqrt(var + EPS)
        emb[z, y, c, k] = jnp.mean(norm.reshape(CN, TOK, D), axis=1).astype(BF)
        go_z(k)
        return carry

    lax.fori_loop(0, CHUNKS, encode, 0)
    go_y(2)
    go_c(1)
    for n in range(2):
        w_fwd_recv(n).wait_recv()
    for n in range(1, 4):
        w_sib(n).start()

    load_tiles().wait()
    for n in range(3):
        id_recv(n).wait_recv()
        tile_recv(n).wait_recv()
    for n in range(QUAD):
        spread[pl.ds(n * TILES * SUB, TILES * SUB), :] = tiles[n].astype(F32).reshape(TILES * SUB, BLK)
    cell = jnp.max(ids[...], axis=0)[0:1, :]
    pick = (lax.broadcasted_iota(jnp.int32, (BLOCKS * BLOCKS, QUAD * TILES), 0) == cell).astype(BF)
    deg[...] = jnp.zeros_like(deg)
    dlane = lax.broadcasted_iota(jnp.int32, (BLOCKS, BLK), 1)

    def place(i, carry):
        rows = spread[pl.ds(i, QUAD * TILES, stride=SUB), :].astype(BF)
        got = jnp.dot(pick, rows, preferred_element_type=F32)
        total = got[:BLOCKS]
        for s in range(BLOCKS):
            part = got[s * BLOCKS:(s + 1) * BLOCKS]
            if s:
                total = total + part
            adj[s, pl.ds(i, BLOCKS, stride=SUB), :] = part
        deg[...] += jnp.where(dlane == i, jnp.sum(total, axis=1, keepdims=True), 0.0)
        return carry

    lax.fori_loop(0, SUB // 2, place, 0)
    go_y(3)
    go_c(2)
    lax.fori_loop(SUB // 2, SUB, place, 0)

    partner = at(z, yoff(2), c)
    d_first = remote(deg, deg_in, d_s.at[0], d_r.at[0], partner)
    d_first.start()
    mine_emb = emb[z, y, c].astype(F32).reshape(NODES, D).astype(BF)
    emb_out[...] = mine_emb
    for h in range(2):
        load_ws(h).wait()
    for n in range(1, 4):
        w_sib_recv(n).wait_recv()
    pre = [jnp.dot(mine_emb, wg[0, n], preferred_element_type=F32) for n in range(NX)]
    d_first.wait_recv()
    deg_sum[...] = deg[...] + deg_in[...]

    def d_send(j):
        return remote(deg_sum, deg_all.at[j], d_s.at[j], d_r.at[j], at(zoff(j), y, c))

    for j in range(1, NZ):
        d_send(j).start()

    go_c(3)
    for k in range(CHUNKS):
        c_recv(k).wait_recv()

    def vy(f):
        return remote(out_y.at[f, :, 1 - yh], in_y.at[f], vy_s.at[f], vy_r.at[f], partner)

    def vz(f, j):
        return remote(out_z.at[f, zoff(j)], in_z.at[f, j], vz_s.at[f, j], vz_r.at[f, j], at(zoff(j), y, c))

    def go_vz(f):
        vy(f).wait_recv()
        both = own[f, :, yh] + in_y[f].astype(F32)
        own[f, :, yh] = both
        out_z[f] = both.astype(BF)
        for j in (4, 3, 5, 2, 6, 1, 7):
            vz(f, j).start()

    a = jnp.concatenate([adj[s].astype(BF) for s in range(BLOCKS)], axis=1)
    for f in range(NFC):
        e = emb[:, :, :, :, :, f * FC:(f + 1) * FC].astype(F32).reshape(NZ * NY * NC * NODES, FC).astype(BF)
        v = jnp.dot(a, e, preferred_element_type=F32).reshape(NZ, 2, SUB, FC)
        own[f] = v
        out_y[f] = v.astype(BF)
        vy(f).start()
        if f:
            go_vz(f - 1)
    go_vz(NFC - 1)

    degree = deg_sum[...]
    for j in range(1, NZ):
        d_send(j).wait_recv()
        degree = degree + deg_all[j]
    block = g // 4
    degree = jnp.sum(
        jnp.where(lax.broadcasted_iota(jnp.int32, (BLOCKS, BLK), 0) == block, degree, 0.0), axis=0, keepdims=True
    )
    on = lax.broadcasted_iota(jnp.int32, (NODES, BLK), 0) == lax.broadcasted_iota(jnp.int32, (NODES, BLK), 1)
    column = jnp.sum(jnp.where(on, jnp.broadcast_to(degree, (NODES, BLK)), 0.0), axis=1, keepdims=True)
    scale = lax.rsqrt(1.0 + column)

    for f in range(NFC):
        total = own[f, z, yh]
        for j in range(1, NZ):
            vz(f, j).wait_recv()
            total = total + in_z[f, j].astype(F32)
        agg = (total * scale).astype(BF)
        for n in range(NX):
            pre[n] = pre[n] + jnp.dot(agg, wg[1, n, f * FC:(f + 1) * FC, :], preferred_element_type=F32)
    act = [jnp.maximum(p, 0.0) for p in pre]
    square = sum(jnp.sum(r * r, axis=1, keepdims=True) for r in act)
    inv = lax.rsqrt(square * (1.0 / HID) + EPS)
    for n in range(NX):
        node_out[:, n * 256:(n + 1) * 256] = (act[n] * inv).astype(BF)

    for n in range(3):
        id_send(n).wait_send()
        tile_send(n).wait_send()
    for n in range(2):
        w_send(n).wait_send()
        w_fwd(n).wait_send()
    for n in range(1, 4):
        w_sib(n).wait_send()
    for k in range(CHUNKS):
        for j in range(1, NZ):
            z_send(k, j).wait_send()
        for j in range(1, NY):
            y_send(k, j).wait_send()
        c_send(k).wait_send()
    d_first.wait_send()
    for j in range(1, NZ):
        d_send(j).wait_send()
    for f in range(NFC):
        vy(f).wait_send()
        for j in range(1, NZ):
            vz(f, j).wait_send()


def on_device(tokens, w_in, w_out, tile_weights, tile_src, tile_dst, w_sage):
    dma = pltpu.SemaphoreType.DMA
    anywhere = pl.BlockSpec(memory_space=pl.ANY)
    smem = pl.BlockSpec(memory_space=pltpu.SMEM)
    vmem = pl.BlockSpec(memory_space=pltpu.VMEM)
    return pl.pallas_call(
        kernel,
        out_shape=(
            jax.ShapeDtypeStruct((NODES, D), BF),
            jax.ShapeDtypeStruct((NODES, HID), BF),
        ),
        in_specs=[anywhere, anywhere, anywhere, anywhere, smem, smem, anywhere],
        out_specs=(vmem, vmem),
        scratch_shapes=[
            pltpu.VMEM((D, FF), BF),
            pltpu.VMEM((FF, D), BF),
            pltpu.VMEM((NODES, TOK, D), BF),
            pltpu.VMEM((QUAD, TILES, SUB, BLK), BF),
            pltpu.VMEM((QUAD, 8, 128), jnp.int32),
            pltpu.VMEM((QUAD * TILES * SUB, BLK), F32),
            pltpu.VMEM((BLOCKS, BLOCKS * SUB, BLK), F32),
            pltpu.VMEM((NZ, NY, NC, CHUNKS, CN, D), BF),
            pltpu.VMEM((2, NX, D, 256), BF),
            pltpu.VMEM((NFC, NZ, 2, SUB, FC), F32),
            pltpu.VMEM((NFC, NZ, 2, SUB, FC), BF),
            pltpu.VMEM((NFC, NZ, SUB, FC), BF),
            pltpu.VMEM((NFC, NZ, SUB, FC), BF),
            pltpu.VMEM((NFC, NZ, SUB, FC), BF),
            pltpu.VMEM((BLOCKS, BLK), F32),
            pltpu.VMEM((BLOCKS, BLK), F32),
            pltpu.VMEM((BLOCKS, BLK), F32),
            pltpu.VMEM((NZ, BLOCKS, BLK), F32),
            dma((15,)),
            dma((3,)), dma((3,)),
            dma((3,)), dma((3,)),
            dma((7,)), dma((7,)),
            dma((CHUNKS, NZ)), dma((CHUNKS, NZ)),
            dma((CHUNKS, NY)), dma((CHUNKS, NY)),
            dma((CHUNKS,)), dma((CHUNKS,)),
            dma((NFC,)), dma((NFC,)),
            dma((NFC, NZ)), dma((NFC, NZ)),
            dma((NZ,)), dma((NZ,)),
        ],
        compiler_params=pltpu.CompilerParams(
            collective_id=0, has_side_effects=True, vmem_limit_bytes=58 * 2**20
        ),
        cost_estimate=pl.CostEstimate(flops=12_000_000_000, bytes_accessed=16_000_000, transcendentals=3_200_000),
        name="encode_and_aggregate",
    )(tokens, w_in, w_out, tile_weights, tile_src, tile_dst, w_sage)


def solution(mesh):
    return jax.shard_map(
        on_device,
        mesh=mesh,
        in_specs=(
            P(("dp", "graph"), None, None),
            P(),
            P(),
            P(("dp", "graph"), None, None),
            P(("dp", "graph")),
            P(("dp", "graph")),
            P(None, "dp"),
        ),
        out_specs=(P(("dp", "graph"), None), P(("dp", "graph"), None)),
        check_vma=False,
    )
```

```python
import functools

import jax
import jax.numpy as jnp
from jax import lax
from jax.experimental import pallas as pl
from jax.experimental.pallas import tpu as pltpu
from jax.sharding import PartitionSpec as P

EPS = 1e-05
MESH = pl.DeviceIdType.MESH

NX, NZ, NY, NC = 4, 8, 4, 2
D, FF, HID = 768, 3072, 1024
BLK, TILES, BLOCKS = 128, 32, 16
NODES, TOK = 32, 32
CHUNKS = 4
CN = NODES // CHUNKS
ROWS = CN * TOK
FB = 768
NFB = FF // FB
QUAD = 4
SUB = BLK // QUAD
FC = 256
NFC = D // FC
UNROLL = 4
ZORDER = (4, 3, 5, 2, 6, 1, 7)
YORDER = (2, 1, 3)
BF, F32 = jnp.bfloat16, jnp.float32


def kernel(
    tok_ref, win_ref, wout_ref, tw_ref, src_ref, dst_ref, ws_ref,
    emb_out, node_out,
    win, wout, tok, tiles, ids, ids_out, spread, adj, adj_t, emb, wg, own, out_y, in_y, out_z, in_z,
    in_z0, out_p, in_p, emb_v, node_v,
    deg, deg_in, deg_sum, deg_all,
    load_sem, tile_s, tile_r, id_s, id_r, w_s, w_r, ag_s, ag_r,
    vy_s, vy_r, vz_s, vz_r, d_s, d_r,
):
    xi = lax.axis_index("dp")
    g = lax.axis_index("graph")
    z, y, c = g // 8, (g // 2) % 4, g % 2
    q = g % 4
    yh = y // 2

    def at(zz, yy, cc):
        return (xi, (zz * NY + yy) * NC + cc)

    def zoff(j):
        return lax.rem(z + j + NZ, NZ)

    def yoff(j):
        return lax.rem(y + j + NY, NY)

    def xoff(j):
        return lax.rem(xi + j + NX, NX)

    def remote(src, dst, ss, rs, dev):
        return pltpu.make_async_remote_copy(
            src_ref=src, dst_ref=dst, send_sem=ss, recv_sem=rs, device_id=dev, device_id_type=MESH
        )

    sib = at(z, y, 1 - c)
    def load_tok(k):
        return pltpu.make_async_copy(tok_ref.at[pl.ds(k * CN, CN)], tok.at[pl.ds(k * CN, CN)], load_sem.at[k])

    def load_in(j):
        cols = pl.ds(j * FB, FB)
        return pltpu.make_async_copy(win_ref.at[:, cols], win.at[:, cols], load_sem.at[4 + j])

    def load_out(j):
        rows = pl.ds(j * FB, FB)
        return pltpu.make_async_copy(wout_ref.at[rows], wout.at[rows], load_sem.at[8 + j])

    def load_tiles():
        return pltpu.make_async_copy(
            tw_ref.at[:, pl.ds(pl.multiple_of(q * SUB, SUB), SUB)], tiles.at[0], load_sem.at[12]
        )

    def load_ws(h):
        return pltpu.make_async_copy(ws_ref.at[pl.ds(h * D, D)], wg.at[h, xi], load_sem.at[13 + h])

    peers = [at(zoff(j), y, c) for j in range(1, NZ)]
    peers += [at(z, yoff(j), c) for j in range(1, NY)]
    peers += [sib, at(z, yoff(1), 1 - c), at(z, yoff(-1), 1 - c), (xoff(1), g), (xoff(-1), g)]
    barrier = pltpu.get_barrier_semaphore()
    for dev in peers:
        pl.semaphore_signal(barrier, inc=1, device_id=dev, device_id_type=MESH)

    load_tok(0).start()
    for j in range(NFB):
        load_in(j).start()
        load_out(j).start()
    for k in range(1, CHUNKS):
        load_tok(k).start()
    load_tiles().start()
    for h in range(2):
        load_ws(h).start()

    low, high = (0, TILES // 2), (TILES // 2, TILES)
    share = [
        (sib, 1, (0, TILES)),
        (at(z, yoff(1), c), 2, low), (at(z, yoff(-1), c), 2, high),
        (at(z, yoff(1), 1 - c), 3, low), (at(z, yoff(-1), 1 - c), 3, high),
    ]

    lane = lax.broadcasted_iota(jnp.int32, (8, 128), 1)
    mine = jnp.full((8, 128), -1, jnp.int32)
    for t in range(TILES):
        mine = jnp.where(lax.rem(lane, TILES) == t, src_ref[t] * BLOCKS + dst_ref[t], mine)
    for n, (slot, (t0, t1)) in enumerate([(0, (0, TILES))] + [e[1:] for e in share]):
        ids_out[n] = jnp.where((lane >= slot * TILES + t0) & (lane < slot * TILES + t1), mine, -1)

    def tile_send(n):
        dev, slot, (t0, t1) = share[n]
        dq = (1 - c if n in (0, 3, 4) else c) + 2 * ((y % 2) if n == 0 else 1 - y % 2)
        part = pl.ds(t0, t1 - t0)
        return remote(tw_ref.at[part, pl.ds(pl.multiple_of(dq * SUB, SUB), SUB)], tiles.at[slot, part],
                      tile_s.at[0], tile_r.at[0], dev)

    def tile_all():
        slot = tiles.at[pl.ds(1, 3)]
        return remote(slot, slot, tile_s.at[0], tile_r.at[0], sib)

    def id_send(n):
        return remote(ids_out.at[n + 1], ids.at[n], id_s.at[0], id_r.at[0], share[n][0])

    def id_all():
        return remote(ids, ids, id_s.at[0], id_r.at[0], sib)

    half = pl.ds(pl.multiple_of(c * D, D), D)

    def w_send(n):
        return remote(ws_ref.at[half], wg.at[c, xi], w_s.at[n], w_r.at[n], (xoff(1 - 2 * n), g))

    def w_recv(n):
        slot = wg.at[c, xoff(2 * n - 1)]
        return remote(slot, slot, w_s.at[n], w_r.at[n], (xoff(1 - 2 * n), g))

    def w_fwd(n):
        rows = pl.ds(n * (D // 2), D // 2)
        slot = wg.at[c, xoff(2 * n - 1), rows]
        return remote(slot, slot, w_s.at[2 + n], w_r.at[2 + n], (xoff(1 - 2 * n), g))

    def w_fwd_recv(n):
        rows = pl.ds(n * (D // 2), D // 2)
        slot = wg.at[c, xoff(2), rows]
        return remote(slot, slot, w_s.at[2 + n], w_r.at[2 + n], (xoff(1 - 2 * n), g))

    def w_sib(n):
        slot = wg.at[c, xoff(n)]
        return remote(slot, slot, w_s.at[3 + n], w_r.at[3 + n], sib)

    def w_sib_recv(n):
        slot = wg.at[1 - c, xoff(n)]
        return remote(slot, slot, w_s.at[3 + n], w_r.at[3 + n], sib)

    def meet():
        pl.semaphore_wait(barrier, len(peers))
        for n in range(len(share)):
            id_send(n).start()
            tile_send(n).start()
        for n in range(2):
            w_send(n).start()

    def z1(k, j=None):
        slot = emb.at[pl.ds(0, NZ - 1) if j is None else z, y, c, k]
        return remote(slot, slot, ag_s.at[0, k], ag_r.at[0, k], at(zoff(j or 1), y, c))

    def y2(k, j=None):
        slot = emb.at[:, pl.ds(0, NY - 1) if j is None else y, c, k]
        return remote(slot, slot, ag_s.at[1, k], ag_r.at[1, k], at(z, yoff(j or 1), c))

    def c_send(k):
        slot = emb.at[:, :, c, k]
        return remote(slot, slot, ag_s.at[2, k], ag_r.at[2, k], sib)

    def c_recv(k):
        slot = emb.at[:, :, 1 - c, k]
        return remote(slot, slot, ag_s.at[2, k], ag_r.at[2, k], sib)

    def go_a(k):
        for j in ZORDER:
            z1(k, j).start()

    def go_b(k):
        z1(k).wait_recv()
        for j in YORDER:
            y2(k, j).start()

    def go_c(k):
        y2(k).wait_recv()
        c_send(k).start()

    def left(k):
        for copies in (y2(k), z1(k), c_send(k)):
            copies.wait_send()

    def encode(k, carry):
        head = carry is None
        load_tok(k).wait()
        x = tok[pl.ds(k * CN, CN)].reshape(ROWS, D)
        acc = x.astype(F32)
        for j in range(NFB):
            if head:
                load_in(j).wait()
                load_out(j).wait()
            h = jnp.dot(x, win[:, j * FB:(j + 1) * FB], preferred_element_type=F32)
            a = (h * 0.5 * (1.0 + lax.erf(h * 0.7071067811865476))).astype(BF)
            acc = acc + jnp.dot(a, wout[j * FB:(j + 1) * FB, :], preferred_element_type=F32)
            if j == 1 and head:
                meet()
            if j == 2 and not head:
                @pl.when(k >= 2)
                def _():
                    go_b(k - 2)
        cent = acc - jnp.mean(acc, axis=1, keepdims=True)
        var = jnp.mean(cent * cent, axis=1, keepdims=True)
        norm = cent * lax.rsqrt(var + EPS)
        emb[z, y, c, k] = jnp.mean(norm.reshape(CN, TOK, D), axis=1).astype(BF)

        go_a(k)
        return carry

    encode(0, None)
    lax.fori_loop(1, CHUNKS, encode, 0)
    for n in range(2):
        w_recv(n).wait_recv()
        w_fwd(n).start()
    go_b(2)

    load_tiles().wait()
    id_all().wait_recv()
    tile_all().wait_recv()
    for n in range(QUAD):
        spread[pl.ds(n * TILES * SUB, TILES * SUB), :] = tiles[n].astype(F32).reshape(TILES * SUB, BLK)
    cell = jnp.maximum(jnp.max(ids[...], axis=0), ids_out[0])[0:1, :]
    pick = (lax.broadcasted_iota(jnp.int32, (BLOCKS * BLOCKS, QUAD * TILES), 0) == cell).astype(BF)
    dlane = lax.broadcasted_iota(jnp.int32, (BLOCKS, BLK), 1)

    def place(n, found):
        for u in range(UNROLL):
            i = n * UNROLL + u
            rows = spread[pl.ds(i, QUAD * TILES, stride=SUB), :].astype(BF)
            got = jnp.dot(pick, rows, preferred_element_type=F32)
            total = got[:BLOCKS]
            to = pl.ds(pl.multiple_of(i * BLOCKS, BLOCKS), BLOCKS)
            for s in range(BLOCKS):
                part = got[s * BLOCKS:(s + 1) * BLOCKS]
                if s:
                    total = total + part
                adj[to, s * BLK:(s + 1) * BLK] = part.astype(BF)
            found = found + jnp.where(dlane == i, jnp.sum(total, axis=1, keepdims=True), 0.0)
        return found

    deg[...] = lax.fori_loop(0, SUB // UNROLL, place, jnp.zeros((BLOCKS, BLK), F32))

    partner = at(z, yoff(2), c)
    d_first = remote(deg, deg_in, d_s.at[0], d_r.at[0], partner)
    d_first.start()
    go_b(3)
    for n in range(2):
        w_fwd_recv(n).wait_recv()
    for n in range(1, 4):
        w_sib(n).start()
    total_rows = BLOCKS * SUB
    r = lax.broadcasted_iota(jnp.int32, (total_rows, total_rows), 0)
    col = lax.broadcasted_iota(jnp.int32, (total_rows, total_rows), 1)
    turn = (col == lax.rem(r, SUB) * BLOCKS + r // SUB).astype(BF)
    for n in range(4):
        cols = slice(n * 512, (n + 1) * 512)
        adj_t[:, cols] = jnp.dot(turn, adj[:, cols], preferred_element_type=F32).astype(BF)
    go_c(0)
    go_c(1)
    emb_v[...] = emb[z, y, c].astype(F32).reshape(NODES, D).astype(BF)
    save_emb = pltpu.make_async_copy(emb_v, emb_out, load_sem.at[15])
    save_emb.start()
    go_c(2)
    d_first.wait_recv()
    deg_sum[...] = deg[...] + deg_in[...]

    def d_send(j):
        return remote(deg_sum, deg_all.at[j], d_s.at[1], d_r.at[1], at(zoff(j), y, c))

    def d_all():
        slot = deg_all.at[pl.ds(1, NZ - 1)]
        return remote(slot, slot, d_s.at[1], d_r.at[1], sib)

    for j in range(1, NZ):
        d_send(j).start()

    go_c(3)
    for k in range(CHUNKS):
        c_recv(k).wait_recv()

    def vy(f):
        if f:
            src, dst = out_y.at[f, :, 1 - yh], in_y.at[f]
        else:
            src, dst = out_p, in_p
        return remote(src, dst, vy_s.at[f], vy_r.at[f], partner)

    def vz(f, j):
        if f:
            src, dst = out_z.at[f, zoff(j)], in_z.at[f, j]
        else:
            src, dst = out_y.at[0, zoff(j)], in_z0.at[j]
        return remote(src, dst, vz_s.at[f], vz_r.at[f], at(zoff(j), y, c))

    def vz_all(f):
        slot = in_z.at[f, pl.ds(1, NZ - 1)] if f else in_z0.at[pl.ds(1, NZ - 1)]
        return remote(slot, slot, vz_s.at[f], vz_r.at[f], sib)

    def go_vz(f):
        vy(f).wait_recv()
        both = own[f, :, yh] + in_y[f].astype(F32)
        own[f, :, yh] = both
        out_z[f] = both.astype(BF)
        for j in ZORDER:
            vz(f, j).start()

    for f in range(NFC):
        e = emb[:, :, :, :, :, f * FC:(f + 1) * FC].astype(F32).reshape(NZ * NY * NC * NODES, FC).astype(BF)
        v = jnp.dot(adj_t[...], e, preferred_element_type=F32).reshape(NZ, 2, SUB, FC)
        own[f] = v
        out_y[f] = v.astype(BF)
        if f:
            vy(f).start()
        else:
            for j in ZORDER:
                vz(0, j).start()
    id_all().wait_send()
    tile_all().wait_send()
    for n in range(2):
        w_send(n).wait_send()
        w_fwd(n).wait_send()
    for n in range(1, 4):
        w_sib(n).wait_send()

    def gone(k, carry):
        left(k)
        return carry

    lax.fori_loop(0, CHUNKS, gone, 0)
    d_first.wait_send()
    d_all().wait_send()

    for h in range(2):
        load_ws(h).wait()
    for n in range(1, 4):
        w_sib_recv(n).wait_recv()
    mine_emb = emb_v[...]
    pre = [jnp.dot(mine_emb, wg[0, n], preferred_element_type=F32) for n in range(NX)]

    go_vz(1)
    vz_all(0).wait_recv()
    for h in range(2):
        total = own[0, z, h]
        for j in range(1, NZ):
            total = total + in_z0[j, h].astype(F32)
        own[0, z, h] = total
    out_p[...] = own[0, z, 1 - yh].astype(BF)
    vy(0).start()
    go_vz(2)

    degree = deg_sum[...]
    d_all().wait_recv()
    for j in range(1, NZ):
        degree = degree + deg_all[j]
    block = g // 4
    degree = jnp.sum(
        jnp.where(lax.broadcasted_iota(jnp.int32, (BLOCKS, BLK), 0) == block, degree, 0.0), axis=0, keepdims=True
    )
    on = lax.broadcasted_iota(jnp.int32, (NODES, BLK), 0) == lax.broadcasted_iota(jnp.int32, (NODES, BLK), 1)
    column = jnp.sum(jnp.where(on, jnp.broadcast_to(degree, (NODES, BLK)), 0.0), axis=1, keepdims=True)
    scale = lax.rsqrt(1.0 + column)

    for f in range(NFC):
        total = own[f, z, yh]
        if f:
            vz_all(f).wait_recv()
            for j in range(1, NZ):
                total = total + in_z[f, j].astype(F32)
        else:
            vy(0).wait_recv()
            total = total + in_p[...].astype(F32)
        agg = (total * scale).astype(BF)
        for n in range(NX):
            pre[n] = pre[n] + jnp.dot(agg, wg[1, n, f * FC:(f + 1) * FC, :], preferred_element_type=F32)
    act = [jnp.maximum(p, 0.0) for p in pre]
    square = sum(jnp.sum(r * r, axis=1, keepdims=True) for r in act)
    inv = lax.rsqrt(square * (1.0 / HID) + EPS)
    for n in range(NX):
        node_v[:, n * 256:(n + 1) * 256] = (act[n] * inv).astype(BF)
    save_node = pltpu.make_async_copy(node_v, node_out, load_sem.at[16])
    save_node.start()

    save_emb.wait()
    save_node.wait()
    for f in range(NFC):
        vy(f).wait_send()
        vz_all(f).wait_send()


def on_device(tokens, w_in, w_out, tile_weights, tile_src, tile_dst, w_sage):
    dma = pltpu.SemaphoreType.DMA
    anywhere = pl.BlockSpec(memory_space=pl.ANY)
    smem = pl.BlockSpec(memory_space=pltpu.SMEM)
    shapes = (jax.ShapeDtypeStruct((NODES, D), BF), jax.ShapeDtypeStruct((NODES, HID), BF))
    return pl.pallas_call(
        kernel,
        out_shape=shapes,
        in_specs=[anywhere, anywhere, anywhere, anywhere, smem, smem, anywhere],
        out_specs=(anywhere, anywhere),
        scratch_shapes=[
            pltpu.VMEM((D, FF), BF),
            pltpu.VMEM((FF, D), BF),
            pltpu.VMEM((NODES, TOK, D), BF),
            pltpu.VMEM((QUAD, TILES, SUB, BLK), BF),
            pltpu.VMEM((5, 8, 128), jnp.int32),
            pltpu.VMEM((6, 8, 128), jnp.int32),
            pltpu.VMEM((QUAD * TILES * SUB, BLK), F32),
            pltpu.VMEM((BLOCKS * SUB, BLOCKS * BLK), BF),
            pltpu.VMEM((BLOCKS * SUB, BLOCKS * BLK), BF),
            pltpu.VMEM((NZ, NY, NC, CHUNKS, CN, D), BF),
            pltpu.VMEM((2, NX, D, 256), BF),
            pltpu.VMEM((NFC, NZ, 2, SUB, FC), F32),
            pltpu.VMEM((NFC, NZ, 2, SUB, FC), BF),
            pltpu.VMEM((NFC, NZ, SUB, FC), BF),
            pltpu.VMEM((NFC, NZ, SUB, FC), BF),
            pltpu.VMEM((NFC, NZ, SUB, FC), BF),
            pltpu.VMEM((NZ, 2, SUB, FC), BF),
            pltpu.VMEM((SUB, FC), BF),
            pltpu.VMEM((SUB, FC), BF),
            pltpu.VMEM((NODES, D), BF),
            pltpu.VMEM((NODES, HID), BF),
            pltpu.VMEM((BLOCKS, BLK), F32),
            pltpu.VMEM((BLOCKS, BLK), F32),
            pltpu.VMEM((BLOCKS, BLK), F32),
            pltpu.VMEM((NZ, BLOCKS, BLK), F32),
            dma((17,)),
            dma((1,)), dma((1,)),
            dma((1,)), dma((1,)),
            dma((7,)), dma((7,)),
            dma((3, CHUNKS)), dma((3, CHUNKS)),
            dma((NFC,)), dma((NFC,)),
            dma((NFC,)), dma((NFC,)),
            dma((2,)), dma((2,)),
        ],
        compiler_params=pltpu.CompilerParams(
            collective_id=0, has_side_effects=True, vmem_limit_bytes=58 * 2**20
        ),
        cost_estimate=pl.CostEstimate(flops=12_000_000_000, bytes_accessed=16_000_000, transcendentals=3_200_000),
        name="encode_and_aggregate",
    )(tokens, w_in, w_out, tile_weights, tile_src, tile_dst, w_sage)


def solution(mesh):
    return jax.shard_map(
        on_device,
        mesh=mesh,
        in_specs=(
            P(("dp", "graph"), None, None),
            P(),
            P(),
            P(("dp", "graph"), None, None),
            P(("dp", "graph")),
            P(("dp", "graph")),
            P(None, "dp"),
        ),
        out_specs=(P(("dp", "graph"), None), P(("dp", "graph"), None)),
        check_vma=False,
    )
```

```python
import functools

import jax
import jax.numpy as jnp
from jax import lax
from jax.experimental import pallas as pl
from jax.experimental.pallas import tpu as pltpu
from jax.sharding import PartitionSpec as P

EPS = 1e-05
MESH = pl.DeviceIdType.MESH

NX, NZ, NY, NC = 4, 8, 4, 2
D, FF, HID = 768, 3072, 1024
BLK, TILES, BLOCKS = 128, 32, 16
NODES, TOK = 32, 32
CHUNKS = 4
CN = NODES // CHUNKS
ROWS = CN * TOK
FB = 768
NFB = FF // FB
QUAD = 4
SUB = BLK // QUAD
FC = 256
NFC = D // FC
PW = FC // 2
NP = D // PW
FIRST_Z = 1
POLL = (0, 2, 1, 3, 4, 5)
UNROLL = 4
ZORDER = (4, 3, 5, 2, 6, 1, 7)
BF, F32 = jnp.bfloat16, jnp.float32


def kernel(
    tok_ref, win_ref, wout_ref, tw_ref, src_ref, dst_ref, ws_ref,
    emb_out, node_out,
    win, wout, tok, tiles, ids, ids_out, spread, adj, adj_t, emb, wg, own, out_y, in_y, out_z, in_z,
    in_z0, out_p, in_p, emb_v, node_v,
    deg, deg_in, deg_sum, deg_all,
    load_sem, tile_s, tile_r, id_s, id_r, w_s, w_r, ag_s, ag_r,
    vy_s, vy_r, vz_s, vz_r, d_s, d_r,
):
    xi = lax.axis_index("dp")
    g = lax.axis_index("graph")
    z, y, c = g // 8, (g // 2) % 4, g % 2
    q = g % 4
    yh = y // 2

    def at(zz, yy, cc):
        return (xi, (zz * NY + yy) * NC + cc)

    def zoff(j):
        return lax.rem(z + j + NZ, NZ)

    def yoff(j):
        return lax.rem(y + j + NY, NY)

    def xoff(j):
        return lax.rem(xi + j + NX, NX)

    def remote(src, dst, ss, rs, dev):
        return pltpu.make_async_remote_copy(
            src_ref=src, dst_ref=dst, send_sem=ss, recv_sem=rs, device_id=dev, device_id_type=MESH
        )

    sib = at(z, y, 1 - c)
    def load_tok(k):
        return pltpu.make_async_copy(tok_ref.at[pl.ds(k * CN, CN)], tok.at[pl.ds(k * CN, CN)], load_sem.at[k])

    def load_in(j):
        cols = pl.ds(j * FB, FB)
        return pltpu.make_async_copy(win_ref.at[:, cols], win.at[:, cols], load_sem.at[4 + j])

    def load_out(j):
        rows = pl.ds(j * FB, FB)
        return pltpu.make_async_copy(wout_ref.at[rows], wout.at[rows], load_sem.at[8 + j])

    def load_tiles():
        return pltpu.make_async_copy(
            tw_ref.at[:, pl.ds(pl.multiple_of(q * SUB, SUB), SUB)], tiles.at[0], load_sem.at[12]
        )

    def load_ws(h):
        return pltpu.make_async_copy(ws_ref.at[pl.ds(h * D, D)], wg.at[h, xi], load_sem.at[13 + h])

    peers = [at(zoff(j), y, c) for j in range(1, NZ)]
    peers += [at(z, yoff(j), c) for j in range(1, NY)]
    peers += [sib, at(z, yoff(1), 1 - c), at(z, yoff(-1), 1 - c), (xoff(1), g), (xoff(-1), g)]
    barrier = pltpu.get_barrier_semaphore()
    for dev in peers:
        pl.semaphore_signal(barrier, inc=1, device_id=dev, device_id_type=MESH)

    load_tok(0).start()
    for j in range(NFB):
        load_in(j).start()
        load_out(j).start()
    for k in range(1, CHUNKS):
        load_tok(k).start()
    load_tiles().start()
    for h in range(2):
        load_ws(h).start()

    low, high = (0, TILES // 2), (TILES // 2, TILES)
    share = [
        (sib, 1, (0, TILES)),
        (at(z, yoff(1), c), 2, low), (at(z, yoff(-1), c), 2, high),
        (at(z, yoff(1), 1 - c), 3, low), (at(z, yoff(-1), 1 - c), 3, high),
    ]

    lane = lax.broadcasted_iota(jnp.int32, (8, 128), 1)
    mine = jnp.full((8, 128), -1, jnp.int32)
    for t in range(TILES):
        mine = jnp.where(lax.rem(lane, TILES) == t, src_ref[t] * BLOCKS + dst_ref[t], mine)
    for n, (slot, (t0, t1)) in enumerate([(0, (0, TILES))] + [e[1:] for e in share]):
        ids_out[n] = jnp.where((lane >= slot * TILES + t0) & (lane < slot * TILES + t1), mine, -1)

    def tile_send(n):
        dev, slot, (t0, t1) = share[n]
        dq = (1 - c if n in (0, 3, 4) else c) + 2 * ((y % 2) if n == 0 else 1 - y % 2)
        part = pl.ds(t0, t1 - t0)
        return remote(tw_ref.at[part, pl.ds(pl.multiple_of(dq * SUB, SUB), SUB)], tiles.at[slot, part],
                      tile_s.at[0], tile_r.at[0], dev)

    def tile_all():
        slot = tiles.at[pl.ds(1, 3)]
        return remote(slot, slot, tile_s.at[0], tile_r.at[0], sib)

    def id_send(n):
        return remote(ids_out.at[n + 1], ids.at[n], id_s.at[0], id_r.at[0], share[n][0])

    def id_all():
        return remote(ids, ids, id_s.at[0], id_r.at[0], sib)

    half = pl.ds(pl.multiple_of(c * D, D), D)

    def w_send(n):
        return remote(ws_ref.at[half], wg.at[c, xi], w_s.at[n], w_r.at[n], (xoff(1 - 2 * n), g))

    def w_recv(n):
        slot = wg.at[c, xoff(2 * n - 1)]
        return remote(slot, slot, w_s.at[n], w_r.at[n], (xoff(1 - 2 * n), g))

    def w_fwd(n):
        rows = pl.ds(n * (D // 2), D // 2)
        slot = wg.at[c, xoff(2 * n - 1), rows]
        return remote(slot, slot, w_s.at[2 + n], w_r.at[2 + n], (xoff(1 - 2 * n), g))

    def w_fwd_recv(n):
        rows = pl.ds(n * (D // 2), D // 2)
        slot = wg.at[c, xoff(2), rows]
        return remote(slot, slot, w_s.at[2 + n], w_r.at[2 + n], (xoff(1 - 2 * n), g))

    def w_sib(n):
        slot = wg.at[c, xoff(n)]
        return remote(slot, slot, w_s.at[3 + n], w_r.at[3 + n], sib)

    def w_sib_recv(n):
        slot = wg.at[1 - c, xoff(n)]
        return remote(slot, slot, w_s.at[3 + n], w_r.at[3 + n], sib)

    def meet():
        pl.semaphore_wait(barrier, len(peers))
        for n in range(len(share)):
            id_send(n).start()
            tile_send(n).start()
        for n in range(2):
            w_send(n).start()

    def z1(k, j=None):
        slot = emb.at[pl.ds(0, NZ - 1) if j is None else z, y, c, k]
        return remote(slot, slot, ag_s.at[0, k], ag_r.at[0, k], at(zoff(j or 1), y, c))

    def ya(k, n, got=False):
        slot = emb.at[:, yoff(2 * n - 1) if got else y, c, k]
        return remote(slot, slot, ag_s.at[1 + n, k], ag_r.at[1 + n, k], at(z, yoff(1 - 2 * n), c))

    def yb(k, n, got=False):
        slot = emb.at[pl.ds(n * (NZ // 2), NZ // 2), yoff(2 if got else 2 * n - 1), c, k]
        return remote(slot, slot, ag_s.at[3 + n, k], ag_r.at[3 + n, k], at(z, yoff(1 - 2 * n), c))

    def c_send(k):
        slot = emb.at[:, :, c, k]
        return remote(slot, slot, ag_s.at[5, k], ag_r.at[5, k], sib)

    def c_recv(k):
        slot = emb.at[:, :, 1 - c, k]
        return remote(slot, slot, ag_s.at[5, k], ag_r.at[5, k], sib)

    def go_a(k):
        for j in ZORDER:
            z1(k, j).start()

    def go_b(k):
        z1(k).wait_recv()
        for n in range(2):
            ya(k, n).start()

    def go_d(k):
        for n in range(2):
            ya(k, n, True).wait_recv()
            yb(k, n).start()

    def go_c(k):
        for n in range(2):
            yb(k, n, True).wait_recv()
        c_send(k).start()

    def left(k):
        for copies in (z1(k), ya(k, 0), ya(k, 1), yb(k, 0), yb(k, 1), c_send(k)):
            copies.wait_send()

    def encode(k, carry):
        head = carry is None
        load_tok(k).wait()
        x = tok[pl.ds(k * CN, CN)].reshape(ROWS, D)
        acc = x.astype(F32)
        for j in range(NFB):
            if head:
                load_in(j).wait()
                load_out(j).wait()
            h = jnp.dot(x, win[:, j * FB:(j + 1) * FB], preferred_element_type=F32)
            a = (h * 0.5 * (1.0 + lax.erf(h * 0.7071067811865476))).astype(BF)
            acc = acc + jnp.dot(a, wout[j * FB:(j + 1) * FB, :], preferred_element_type=F32)
            if j == 1 and head:
                meet()
            if j == 1 and not head:
                @pl.when(k >= 2)
                def _():
                    go_b(k - 2)
        cent = acc - jnp.mean(acc, axis=1, keepdims=True)
        var = jnp.mean(cent * cent, axis=1, keepdims=True)
        norm = cent * lax.rsqrt(var + EPS)
        emb[z, y, c, k] = jnp.mean(norm.reshape(CN, TOK, D), axis=1).astype(BF)

        go_a(k)
        return carry

    encode(0, None)
    lax.fori_loop(1, CHUNKS, encode, 0)
    for n in range(2):
        w_recv(n).wait_recv()
        w_fwd(n).start()
    go_d(0)
    go_b(2)

    load_tiles().wait()
    id_all().wait_recv()
    tile_all().wait_recv()
    for n in range(QUAD):
        spread[pl.ds(n * TILES * SUB, TILES * SUB), :] = tiles[n].astype(F32).reshape(TILES * SUB, BLK)
    cell = jnp.maximum(jnp.max(ids[...], axis=0), ids_out[0])[0:1, :]
    pick = (lax.broadcasted_iota(jnp.int32, (BLOCKS * BLOCKS, QUAD * TILES), 0) == cell).astype(BF)
    dlane = lax.broadcasted_iota(jnp.int32, (BLOCKS, BLK), 1)

    def place(n, found):
        for u in range(UNROLL):
            i = n * UNROLL + u
            rows = spread[pl.ds(i, QUAD * TILES, stride=SUB), :].astype(BF)
            got = jnp.dot(pick, rows, preferred_element_type=F32)
            total = got[:BLOCKS]
            to = pl.ds(pl.multiple_of(i * BLOCKS, BLOCKS), BLOCKS)
            for s in range(BLOCKS):
                part = got[s * BLOCKS:(s + 1) * BLOCKS]
                if s:
                    total = total + part
                adj[to, s * BLK:(s + 1) * BLK] = part.astype(BF)
            found = found + jnp.where(dlane == i, jnp.sum(total, axis=1, keepdims=True), 0.0)
        return found

    steps = SUB // UNROLL
    found = lax.fori_loop(0, steps // 2, place, jnp.zeros((BLOCKS, BLK), F32))
    go_d(1)
    deg[...] = lax.fori_loop(steps // 2, steps, place, found)

    partner = at(z, yoff(2), c)
    d_first = remote(deg, deg_in, d_s.at[0], d_r.at[0], partner)
    d_first.start()
    go_b(3)
    go_d(2)
    total_rows = BLOCKS * SUB
    r = lax.broadcasted_iota(jnp.int32, (total_rows, total_rows), 0)
    col = lax.broadcasted_iota(jnp.int32, (total_rows, total_rows), 1)
    turn = (col == lax.rem(r, SUB) * BLOCKS + r // SUB).astype(BF)
    for n in range(4):
        cols = slice(n * 512, (n + 1) * 512)
        adj_t[:, cols] = jnp.dot(turn, adj[:, cols], preferred_element_type=F32).astype(BF)
    go_c(0)
    go_c(1)
    emb_v[...] = emb[z, y, c].astype(F32).reshape(NODES, D).astype(BF)
    save_emb = pltpu.make_async_copy(emb_v, emb_out, load_sem.at[15])
    save_emb.start()
    go_d(3)
    go_c(2)
    for n in range(2):
        w_fwd_recv(n).wait_recv()
    for n in range(1, 4):
        w_sib(n).start()
    d_first.wait_recv()
    deg_sum[...] = deg[...] + deg_in[...]

    def d_send(j):
        return remote(deg_sum, deg_all.at[j], d_s.at[1], d_r.at[1], at(zoff(j), y, c))

    def d_all():
        slot = deg_all.at[pl.ds(1, NZ - 1)]
        return remote(slot, slot, d_s.at[1], d_r.at[1], sib)

    for j in range(1, NZ):
        d_send(j).start()

    go_c(3)
    for k in range(CHUNKS):
        c_recv(k).wait_recv()

    def lanes(p):
        return pl.ds(p % 2 * PW, PW)

    def vy(p):
        if p == FIRST_Z:
            src, dst = out_p, in_p
        else:
            src, dst = out_y.at[p // 2, :, 1 - yh, :, lanes(p)], in_y.at[p]
        return remote(src, dst, vy_s.at[p], vy_r.at[p], partner)

    def vz(p, j):
        if p == FIRST_Z:
            src, dst = out_y.at[p // 2, zoff(j), :, :, lanes(p)], in_z0.at[j]
        else:
            src, dst = out_z.at[p, zoff(j)], in_z.at[p, j]
        return remote(src, dst, vz_s.at[p], vz_r.at[p], at(zoff(j), y, c))

    def vz_all(p):
        slot = in_z0.at[pl.ds(1, NZ - 1)] if p == FIRST_Z else in_z.at[p, pl.ds(1, NZ - 1)]
        return remote(slot, slot, vz_s.at[p], vz_r.at[p], sib)

    def go_vz(p):
        if p == FIRST_Z:
            vz_all(p).wait_recv()
            for h in range(2):
                total = own[p // 2, z, h, :, lanes(p)]
                for j in range(1, NZ):
                    total = total + in_z0[j, h].astype(F32)
                own[p // 2, z, h, :, lanes(p)] = total
            out_p[...] = own[p // 2, z, 1 - yh, :, lanes(p)].astype(BF)
            vy(p).start()
            return
        vy(p).wait_recv()
        both = own[p // 2, :, yh, :, lanes(p)] + in_y[p].astype(F32)
        own[p // 2, :, yh, :, lanes(p)] = both
        out_z[p] = both.astype(BF)
        for j in ZORDER:
            vz(p, j).start()

    for f in range(NFC):
        e = emb[:, :, :, :, :, f * FC:(f + 1) * FC].astype(F32).reshape(NZ * NY * NC * NODES, FC).astype(BF)
        v = jnp.dot(adj_t[...], e, preferred_element_type=F32).reshape(NZ, 2, SUB, FC)
        own[f] = v
        out_y[f] = v.astype(BF)
        for p in (2 * f, 2 * f + 1):
            if p == FIRST_Z:
                for j in ZORDER:
                    vz(p, j).start()
            else:
                vy(p).start()
    id_all().wait_send()
    tile_all().wait_send()
    for n in range(2):
        w_send(n).wait_send()
        w_fwd(n).wait_send()
    for n in range(1, 4):
        w_sib(n).wait_send()

    def gone(k, carry):
        left(k)
        return carry

    lax.fori_loop(0, CHUNKS, gone, 0)
    d_first.wait_send()
    d_all().wait_send()

    for h in range(2):
        load_ws(h).wait()
    for n in range(1, 4):
        w_sib_recv(n).wait_recv()
    mine_emb = emb_v[...]
    pre = [jnp.dot(mine_emb, wg[0, n], preferred_element_type=F32) for n in range(NX)]

    for p in POLL:
        go_vz(p)

    degree = deg_sum[...]
    d_all().wait_recv()
    for j in range(1, NZ):
        degree = degree + deg_all[j]
    block = g // 4
    degree = jnp.sum(
        jnp.where(lax.broadcasted_iota(jnp.int32, (BLOCKS, BLK), 0) == block, degree, 0.0), axis=0, keepdims=True
    )
    on = lax.broadcasted_iota(jnp.int32, (NODES, BLK), 0) == lax.broadcasted_iota(jnp.int32, (NODES, BLK), 1)
    column = jnp.sum(jnp.where(on, jnp.broadcast_to(degree, (NODES, BLK)), 0.0), axis=1, keepdims=True)
    scale = lax.rsqrt(1.0 + column)

    for f in range(NFC):
        sides = []
        for p in (2 * f, 2 * f + 1):
            total = own[f, z, yh, :, lanes(p)]
            if p == FIRST_Z:
                vy(p).wait_recv()
                total = total + in_p[...].astype(F32)
            else:
                vz_all(p).wait_recv()
                for j in range(1, NZ):
                    total = total + in_z[p, j].astype(F32)
            sides.append((total * scale).astype(BF))
        agg = jnp.concatenate(sides, axis=1)
        for n in range(NX):
            pre[n] = pre[n] + jnp.dot(agg, wg[1, n, f * FC:(f + 1) * FC, :], preferred_element_type=F32)
    act = [jnp.maximum(p, 0.0) for p in pre]
    square = sum(jnp.sum(r * r, axis=1, keepdims=True) for r in act)
    inv = lax.rsqrt(square * (1.0 / HID) + EPS)
    for n in range(NX):
        node_v[:, n * 256:(n + 1) * 256] = (act[n] * inv).astype(BF)
    save_node = pltpu.make_async_copy(node_v, node_out, load_sem.at[16])
    save_node.start()

    save_emb.wait()
    save_node.wait()
    for p in range(NP):
        vy(p).wait_send()
        vz_all(p).wait_send()


def on_device(tokens, w_in, w_out, tile_weights, tile_src, tile_dst, w_sage):
    dma = pltpu.SemaphoreType.DMA
    anywhere = pl.BlockSpec(memory_space=pl.ANY)
    smem = pl.BlockSpec(memory_space=pltpu.SMEM)
    shapes = (jax.ShapeDtypeStruct((NODES, D), BF), jax.ShapeDtypeStruct((NODES, HID), BF))
    return pl.pallas_call(
        kernel,
        out_shape=shapes,
        in_specs=[anywhere, anywhere, anywhere, anywhere, smem, smem, anywhere],
        out_specs=(anywhere, anywhere),
        scratch_shapes=[
            pltpu.VMEM((D, FF), BF),
            pltpu.VMEM((FF, D), BF),
            pltpu.VMEM((NODES, TOK, D), BF),
            pltpu.VMEM((QUAD, TILES, SUB, BLK), BF),
            pltpu.VMEM((5, 8, 128), jnp.int32),
            pltpu.VMEM((6, 8, 128), jnp.int32),
            pltpu.VMEM((QUAD * TILES * SUB, BLK), F32),
            pltpu.VMEM((BLOCKS * SUB, BLOCKS * BLK), BF),
            pltpu.VMEM((BLOCKS * SUB, BLOCKS * BLK), BF),
            pltpu.VMEM((NZ, NY, NC, CHUNKS, CN, D), BF),
            pltpu.VMEM((2, NX, D, 256), BF),
            pltpu.VMEM((NFC, NZ, 2, SUB, FC), F32),
            pltpu.VMEM((NFC, NZ, 2, SUB, FC), BF),
            pltpu.VMEM((NP, NZ, SUB, PW), BF),
            pltpu.VMEM((NP, NZ, SUB, PW), BF),
            pltpu.VMEM((NP, NZ, SUB, PW), BF),
            pltpu.VMEM((NZ, 2, SUB, PW), BF),
            pltpu.VMEM((SUB, PW), BF),
            pltpu.VMEM((SUB, PW), BF),
            pltpu.VMEM((NODES, D), BF),
            pltpu.VMEM((NODES, HID), BF),
            pltpu.VMEM((BLOCKS, BLK), F32),
            pltpu.VMEM((BLOCKS, BLK), F32),
            pltpu.VMEM((BLOCKS, BLK), F32),
            pltpu.VMEM((NZ, BLOCKS, BLK), F32),
            dma((17,)),
            dma((1,)), dma((1,)),
            dma((1,)), dma((1,)),
            dma((7,)), dma((7,)),
            dma((6, CHUNKS)), dma((6, CHUNKS)),
            dma((NP,)), dma((NP,)),
            dma((NP,)), dma((NP,)),
            dma((2,)), dma((2,)),
        ],
        compiler_params=pltpu.CompilerParams(
            collective_id=0, has_side_effects=True, vmem_limit_bytes=58 * 2**20
        ),
        cost_estimate=pl.CostEstimate(flops=12_000_000_000, bytes_accessed=16_000_000, transcendentals=3_200_000),
        name="encode_and_aggregate",
    )(tokens, w_in, w_out, tile_weights, tile_src, tile_dst, w_sage)


def solution(mesh):
    return jax.shard_map(
        on_device,
        mesh=mesh,
        in_specs=(
            P(("dp", "graph"), None, None),
            P(),
            P(),
            P(("dp", "graph"), None, None),
            P(("dp", "graph")),
            P(("dp", "graph")),
            P(None, "dp"),
        ),
        out_specs=(P(("dp", "graph"), None), P(("dp", "graph"), None)),
        check_vma=False,
    )
```

```python
import functools

import jax
import jax.numpy as jnp
from jax import lax
from jax.experimental import pallas as pl
from jax.experimental.pallas import tpu as pltpu
from jax.sharding import PartitionSpec as P

EPS = 1e-05
MESH = pl.DeviceIdType.MESH

NX, NZ, NY, NC = 4, 8, 4, 2
D, FF, HID = 768, 3072, 1024
BLK, TILES, BLOCKS = 128, 32, 16
NODES, TOK = 32, 32
CHUNKS = 4
CN = NODES // CHUNKS
ROWS = CN * TOK
FB = 768
NFB = FF // FB
QUAD = 4
SUB = BLK // QUAD
FC = 256
NFC = D // FC
PW = FC // 2
NP = D // PW
FIRST_Z = 1
POLL = (0, 2, 1, 3, 4, 5)
UNROLL = 4
ZORDER = (4, 3, 5, 2, 6, 1, 7)
YORDER = (2, 1, 3)
BF, F32 = jnp.bfloat16, jnp.float32


def kernel(
    tok_ref, win_ref, wout_ref, tw_ref, src_ref, dst_ref, ws_ref,
    emb_out, node_out,
    win, wout, tok, tiles, ids, ids_out, spread, adj, adj_t, emb, wg, own, out_y, in_y, out_z, in_z,
    in_z0, out_p, in_p, emb_v, node_v,
    deg, deg_in, deg_sum, deg_all,
    load_sem, tile_s, tile_r, id_s, id_r, w_s, w_r, ag_s, ag_r,
    vy_s, vy_r, vz_s, vz_r, d_s, d_r,
):
    xi = lax.axis_index("dp")
    g = lax.axis_index("graph")
    z, y, c = g // 8, (g // 2) % 4, g % 2
    q = g % 4
    yh = y // 2

    def at(zz, yy, cc):
        return (xi, (zz * NY + yy) * NC + cc)

    def zoff(j):
        return lax.rem(z + j + NZ, NZ)

    def yoff(j):
        return lax.rem(y + j + NY, NY)

    def xoff(j):
        return lax.rem(xi + j + NX, NX)

    def remote(src, dst, ss, rs, dev):
        return pltpu.make_async_remote_copy(
            src_ref=src, dst_ref=dst, send_sem=ss, recv_sem=rs, device_id=dev, device_id_type=MESH
        )

    sib = at(z, y, 1 - c)
    def load_tok(k):
        return pltpu.make_async_copy(tok_ref.at[pl.ds(k * CN, CN)], tok.at[pl.ds(k * CN, CN)], load_sem.at[k])

    def load_in(j):
        cols = pl.ds(j * FB, FB)
        return pltpu.make_async_copy(win_ref.at[:, cols], win.at[:, cols], load_sem.at[4 + j])

    def load_out(j):
        rows = pl.ds(j * FB, FB)
        return pltpu.make_async_copy(wout_ref.at[rows], wout.at[rows], load_sem.at[8 + j])

    def load_tiles():
        return pltpu.make_async_copy(
            tw_ref.at[:, pl.ds(pl.multiple_of(q * SUB, SUB), SUB)], tiles.at[0], load_sem.at[12]
        )

    def load_ws(h):
        return pltpu.make_async_copy(ws_ref.at[pl.ds(h * D, D)], wg.at[h, xi], load_sem.at[13 + h])

    peers = [at(zoff(j), y, c) for j in range(1, NZ)]
    peers += [at(z, yoff(j), c) for j in range(1, NY)]
    peers += [sib, at(z, yoff(1), 1 - c), at(z, yoff(-1), 1 - c), (xoff(1), g), (xoff(-1), g)]
    barrier = pltpu.get_barrier_semaphore()
    for dev in peers:
        pl.semaphore_signal(barrier, inc=1, device_id=dev, device_id_type=MESH)

    load_tok(0).start()
    for j in range(NFB):
        load_in(j).start()
        load_out(j).start()
    for k in range(1, CHUNKS):
        load_tok(k).start()
    load_tiles().start()
    for h in range(2):
        load_ws(h).start()

    low, high = (0, TILES // 2), (TILES // 2, TILES)
    share = [
        (sib, 1, (0, TILES)),
        (at(z, yoff(1), c), 2, low), (at(z, yoff(-1), c), 2, high),
        (at(z, yoff(1), 1 - c), 3, low), (at(z, yoff(-1), 1 - c), 3, high),
    ]

    lane = lax.broadcasted_iota(jnp.int32, (8, 128), 1)
    mine = jnp.full((8, 128), -1, jnp.int32)
    for t in range(TILES):
        mine = jnp.where(lax.rem(lane, TILES) == t, src_ref[t] * BLOCKS + dst_ref[t], mine)
    for n, (slot, (t0, t1)) in enumerate([(0, (0, TILES))] + [e[1:] for e in share]):
        ids_out[n] = jnp.where((lane >= slot * TILES + t0) & (lane < slot * TILES + t1), mine, -1)

    def tile_send(n):
        dev, slot, (t0, t1) = share[n]
        dq = (1 - c if n in (0, 3, 4) else c) + 2 * ((y % 2) if n == 0 else 1 - y % 2)
        part = pl.ds(t0, t1 - t0)
        return remote(tw_ref.at[part, pl.ds(pl.multiple_of(dq * SUB, SUB), SUB)], tiles.at[slot, part],
                      tile_s.at[0], tile_r.at[0], dev)

    def tile_all():
        slot = tiles.at[pl.ds(1, 3)]
        return remote(slot, slot, tile_s.at[0], tile_r.at[0], sib)

    def id_send(n):
        return remote(ids_out.at[n + 1], ids.at[n], id_s.at[0], id_r.at[0], share[n][0])

    def id_all():
        return remote(ids, ids, id_s.at[0], id_r.at[0], sib)

    half = pl.ds(pl.multiple_of(c * D, D), D)

    def w_send(n):
        return remote(ws_ref.at[half], wg.at[c, xi], w_s.at[n], w_r.at[n], (xoff(1 - 2 * n), g))

    def w_recv(n):
        slot = wg.at[c, xoff(2 * n - 1)]
        return remote(slot, slot, w_s.at[n], w_r.at[n], (xoff(1 - 2 * n), g))

    def w_fwd(n):
        rows = pl.ds(n * (D // 2), D // 2)
        slot = wg.at[c, xoff(2 * n - 1), rows]
        return remote(slot, slot, w_s.at[2 + n], w_r.at[2 + n], (xoff(1 - 2 * n), g))

    def w_fwd_recv(n):
        rows = pl.ds(n * (D // 2), D // 2)
        slot = wg.at[c, xoff(2), rows]
        return remote(slot, slot, w_s.at[2 + n], w_r.at[2 + n], (xoff(1 - 2 * n), g))

    def w_sib(n):
        slot = wg.at[c, xoff(n)]
        return remote(slot, slot, w_s.at[3 + n], w_r.at[3 + n], sib)

    def w_sib_recv(n):
        slot = wg.at[1 - c, xoff(n)]
        return remote(slot, slot, w_s.at[3 + n], w_r.at[3 + n], sib)

    def meet():
        pl.semaphore_wait(barrier, len(peers))
        for n in range(len(share)):
            id_send(n).start()
            tile_send(n).start()
        for n in range(2):
            w_send(n).start()

    def z1(k, j=None):
        slot = emb.at[pl.ds(0, NZ - 1) if j is None else z, y, c, k]
        return remote(slot, slot, ag_s.at[0, k], ag_r.at[0, k], at(zoff(j or 1), y, c))

    def ya(k, n, got=False):
        slot = emb.at[:, yoff(2 * n - 1) if got else y, c, k]
        return remote(slot, slot, ag_s.at[1 + n, k], ag_r.at[1 + n, k], at(z, yoff(1 - 2 * n), c))

    def yb(k, n, got=False):
        slot = emb.at[pl.ds(n * (NZ // 2), NZ // 2), yoff(2 if got else 2 * n - 1), c, k]
        return remote(slot, slot, ag_s.at[3 + n, k], ag_r.at[3 + n, k], at(z, yoff(1 - 2 * n), c))

    end = CHUNKS - 1
    front, back = pl.ds(0, D // 2), pl.ds(D // 2, D // 2)

    def zy1(j=None):
        slot = emb.at[pl.ds(0, NZ - 1) if j is None else z, y, c, end, :, front]
        return remote(slot, slot, ag_s.at[0, end], ag_r.at[0, end], at(zoff(j or 1), y, c))

    def zy2(j=None):
        slot = emb.at[:, pl.ds(0, NY - 1) if j is None else y, c, end, :, front]
        return remote(slot, slot, ag_s.at[1, end], ag_r.at[1, end], at(z, yoff(j or 1), c))

    def yz1(j=None):
        slot = emb.at[z, pl.ds(0, NY - 1) if j is None else y, c, end, :, back]
        return remote(slot, slot, ag_s.at[2, end], ag_r.at[2, end], at(z, yoff(j or 1), c))

    def yz2(j=None):
        slot = emb.at[pl.ds(0, NZ - 1) if j is None else z, :, c, end, :, back]
        return remote(slot, slot, ag_s.at[3, end], ag_r.at[3, end], at(zoff(j or 1), y, c))

    def c_send(k):
        slot = emb.at[:, :, c, k]
        return remote(slot, slot, ag_s.at[5, k], ag_r.at[5, k], sib)

    def c_recv(k):
        slot = emb.at[:, :, 1 - c, k]
        return remote(slot, slot, ag_s.at[5, k], ag_r.at[5, k], sib)

    def go_a(k, last=False):
        if last:
            for j in YORDER:
                yz1(j).start()
            for j in ZORDER:
                zy1(j).start()
            return
        for j in ZORDER:
            z1(k, j).start()

    def go_b(k):
        z1(k).wait_recv()
        for n in range(2):
            ya(k, n).start()

    def go_d(k):
        for n in range(2):
            ya(k, n, True).wait_recv()
            yb(k, n).start()

    def go_e():
        yz1().wait_recv()
        for j in ZORDER:
            yz2(j).start()

    def go_f():
        zy1().wait_recv()
        for j in YORDER:
            zy2(j).start()

    def go_c(k):
        if k < end:
            for n in range(2):
                yb(k, n, True).wait_recv()
        else:
            zy2().wait_recv()
            yz2().wait_recv()
        c_send(k).start()

    def left(k):
        if k < end:
            z1(k).wait_send()
            for n in range(2):
                ya(k, n).wait_send()
                yb(k, n).wait_send()
        else:
            for copies in (zy1, zy2, yz1, yz2):
                copies().wait_send()
        c_send(k).wait_send()

    def encode(k, carry, head=False, last=False):
        load_tok(k).wait()
        x = tok[pl.ds(k * CN, CN)].reshape(ROWS, D)
        acc = x.astype(F32)
        for j in range(NFB):
            if head:
                load_in(j).wait()
                load_out(j).wait()
            h = jnp.dot(x, win[:, j * FB:(j + 1) * FB], preferred_element_type=F32)
            a = (h * 0.5 * (1.0 + lax.erf(h * 0.7071067811865476))).astype(BF)
            acc = acc + jnp.dot(a, wout[j * FB:(j + 1) * FB, :], preferred_element_type=F32)
            if j == 1 and head:
                meet()
            if j == 1 and last:
                go_b(k - 2)
            elif j == 1 and not head:
                @pl.when(k >= 2)
                def _():
                    go_b(k - 2)
        cent = acc - jnp.mean(acc, axis=1, keepdims=True)
        var = jnp.mean(cent * cent, axis=1, keepdims=True)
        norm = cent * lax.rsqrt(var + EPS)
        emb[z, y, c, k] = jnp.mean(norm.reshape(CN, TOK, D), axis=1).astype(BF)

        go_a(k, last)
        return carry

    encode(0, 0, head=True)
    lax.fori_loop(1, end, encode, 0)
    encode(end, 0, last=True)
    for n in range(2):
        w_recv(n).wait_recv()
        w_fwd(n).start()
    go_d(0)
    go_b(2)

    load_tiles().wait()
    id_all().wait_recv()
    tile_all().wait_recv()
    for n in range(QUAD):
        spread[pl.ds(n * TILES * SUB, TILES * SUB), :] = tiles[n].astype(F32).reshape(TILES * SUB, BLK)
    cell = jnp.maximum(jnp.max(ids[...], axis=0), ids_out[0])[0:1, :]
    pick = (lax.broadcasted_iota(jnp.int32, (BLOCKS * BLOCKS, QUAD * TILES), 0) == cell).astype(BF)
    dlane = lax.broadcasted_iota(jnp.int32, (BLOCKS, BLK), 1)

    def place(n, found):
        for u in range(UNROLL):
            i = n * UNROLL + u
            rows = spread[pl.ds(i, QUAD * TILES, stride=SUB), :].astype(BF)
            got = jnp.dot(pick, rows, preferred_element_type=F32)
            total = got[:BLOCKS]
            to = pl.ds(pl.multiple_of(i * BLOCKS, BLOCKS), BLOCKS)
            for s in range(BLOCKS):
                part = got[s * BLOCKS:(s + 1) * BLOCKS]
                if s:
                    total = total + part
                adj[to, s * BLK:(s + 1) * BLK] = part.astype(BF)
            found = found + jnp.where(dlane == i, jnp.sum(total, axis=1, keepdims=True), 0.0)
        return found

    steps = SUB // UNROLL
    found = lax.fori_loop(0, steps // 2, place, jnp.zeros((BLOCKS, BLK), F32))
    go_d(1)
    go_e()
    deg[...] = lax.fori_loop(steps // 2, steps, place, found)

    partner = at(z, yoff(2), c)
    d_first = remote(deg, deg_in, d_s.at[0], d_r.at[0], partner)
    d_first.start()
    go_f()
    go_c(0)
    wide = BLOCKS * SUB
    r = lax.broadcasted_iota(jnp.int32, (wide, wide), 0)
    col = lax.broadcasted_iota(jnp.int32, (wide, wide), 1)
    turn = (col == lax.rem(r, SUB) * BLOCKS + r // SUB).astype(BF)
    place_of = lax.rem(col, BLK) // NODES * BLK + lax.rem(col, NODES) // CN * NODES + col // BLK * CN + lax.rem(col, CN)
    turn_cols = (r == place_of).astype(BF)
    for n in range(4):
        cols = slice(n * wide, (n + 1) * wide)
        turned = jnp.dot(turn, adj[:, cols], preferred_element_type=F32).astype(BF)
        adj_t[:, cols] = jnp.dot(turned, turn_cols, preferred_element_type=F32).astype(BF)
        if n == 1:
            go_d(2)
            go_c(1)
    emb_v[...] = emb[z, y, c].astype(F32).reshape(NODES, D).astype(BF)
    save_emb = pltpu.make_async_copy(emb_v, emb_out, load_sem.at[15])
    save_emb.start()
    for n in range(2):
        w_fwd_recv(n).wait_recv()
    for n in range(1, 4):
        w_sib(n).start()
    d_first.wait_recv()
    deg_sum[...] = deg[...] + deg_in[...]

    def d_send(j):
        return remote(deg_sum, deg_all.at[j], d_s.at[1], d_r.at[1], at(zoff(j), y, c))

    def d_all():
        slot = deg_all.at[pl.ds(1, NZ - 1)]
        return remote(slot, slot, d_s.at[1], d_r.at[1], sib)

    for j in range(1, NZ):
        d_send(j).start()

    def weighted(chunks, f):
        left_side = [
            adj_t[:, n * wide + k * BLK:n * wide + (k + 1) * BLK] for k in chunks for n in range(4)
        ]
        right_side = [
            emb[:, :, :, k, :, f * FC:(f + 1) * FC].astype(F32).reshape(wide, FC).astype(BF) for k in chunks
        ]
        return jnp.dot(
            jnp.concatenate(left_side, axis=1), jnp.concatenate(right_side, axis=0), preferred_element_type=F32
        ).reshape(NZ, 2, SUB, FC)

    go_c(2)
    go_c(3)
    for k in range(2):
        c_recv(k).wait_recv()
    for f in range(NFC):
        own[f] = weighted((0, 1), f)
    for k in range(2, CHUNKS):
        c_recv(k).wait_recv()

    def lanes(p):
        return pl.ds(p % 2 * PW, PW)

    def vy(p):
        if p == FIRST_Z:
            src, dst = out_p, in_p
        else:
            src, dst = out_y.at[p // 2, :, 1 - yh, :, lanes(p)], in_y.at[p]
        return remote(src, dst, vy_s.at[p], vy_r.at[p], partner)

    def vz(p, j):
        if p == FIRST_Z:
            src, dst = out_y.at[p // 2, zoff(j), :, :, lanes(p)], in_z0.at[j]
        else:
            src, dst = out_z.at[p, zoff(j)], in_z.at[p, j]
        return remote(src, dst, vz_s.at[p], vz_r.at[p], at(zoff(j), y, c))

    def vz_all(p):
        slot = in_z0.at[pl.ds(1, NZ - 1)] if p == FIRST_Z else in_z.at[p, pl.ds(1, NZ - 1)]
        return remote(slot, slot, vz_s.at[p], vz_r.at[p], sib)

    def go_vz(p):
        if p == FIRST_Z:
            vz_all(p).wait_recv()
            for h in range(2):
                total = own[p // 2, z, h, :, lanes(p)]
                for j in range(1, NZ):
                    total = total + in_z0[j, h].astype(F32)
                own[p // 2, z, h, :, lanes(p)] = total
            out_p[...] = own[p // 2, z, 1 - yh, :, lanes(p)].astype(BF)
            vy(p).start()
            return
        vy(p).wait_recv()
        both = own[p // 2, :, yh, :, lanes(p)] + in_y[p].astype(F32)
        own[p // 2, :, yh, :, lanes(p)] = both
        out_z[p] = both.astype(BF)
        for j in ZORDER:
            vz(p, j).start()

    for f in range(NFC):
        v = own[f] + weighted((2, 3), f)
        own[f] = v
        out_y[f] = v.astype(BF)
        for p in (2 * f, 2 * f + 1):
            if p == FIRST_Z:
                for j in ZORDER:
                    vz(p, j).start()
            else:
                vy(p).start()
    id_all().wait_send()
    tile_all().wait_send()
    for n in range(2):
        w_send(n).wait_send()
        w_fwd(n).wait_send()
    for n in range(1, 4):
        w_sib(n).wait_send()

    for k in range(CHUNKS):
        left(k)
    d_first.wait_send()
    d_all().wait_send()

    for h in range(2):
        load_ws(h).wait()
    for n in range(1, 4):
        w_sib_recv(n).wait_recv()
    mine_emb = emb_v[...]
    pre = [jnp.dot(mine_emb, wg[0, n], preferred_element_type=F32) for n in range(NX)]

    for p in POLL:
        go_vz(p)

    degree = deg_sum[...]
    d_all().wait_recv()
    for j in range(1, NZ):
        degree = degree + deg_all[j]
    block = g // 4
    degree = jnp.sum(
        jnp.where(lax.broadcasted_iota(jnp.int32, (BLOCKS, BLK), 0) == block, degree, 0.0), axis=0, keepdims=True
    )
    on = lax.broadcasted_iota(jnp.int32, (NODES, BLK), 0) == lax.broadcasted_iota(jnp.int32, (NODES, BLK), 1)
    column = jnp.sum(jnp.where(on, jnp.broadcast_to(degree, (NODES, BLK)), 0.0), axis=1, keepdims=True)
    scale = lax.rsqrt(1.0 + column)

    for f in range(NFC):
        sides = []
        for p in (2 * f, 2 * f + 1):
            total = own[f, z, yh, :, lanes(p)]
            if p == FIRST_Z:
                vy(p).wait_recv()
                total = total + in_p[...].astype(F32)
            else:
                vz_all(p).wait_recv()
                for j in range(1, NZ):
                    total = total + in_z[p, j].astype(F32)
            sides.append((total * scale).astype(BF))
        agg = jnp.concatenate(sides, axis=1)
        for n in range(NX):
            pre[n] = pre[n] + jnp.dot(agg, wg[1, n, f * FC:(f + 1) * FC, :], preferred_element_type=F32)
    act = [jnp.maximum(p, 0.0) for p in pre]
    square = sum(jnp.sum(r * r, axis=1, keepdims=True) for r in act)
    inv = lax.rsqrt(square * (1.0 / HID) + EPS)
    for n in range(NX):
        node_v[:, n * 256:(n + 1) * 256] = (act[n] * inv).astype(BF)
    save_node = pltpu.make_async_copy(node_v, node_out, load_sem.at[16])
    save_node.start()

    save_emb.wait()
    save_node.wait()
    for p in range(NP):
        vy(p).wait_send()
        vz_all(p).wait_send()


def on_device(tokens, w_in, w_out, tile_weights, tile_src, tile_dst, w_sage):
    dma = pltpu.SemaphoreType.DMA
    anywhere = pl.BlockSpec(memory_space=pl.ANY)
    smem = pl.BlockSpec(memory_space=pltpu.SMEM)
    shapes = (jax.ShapeDtypeStruct((NODES, D), BF), jax.ShapeDtypeStruct((NODES, HID), BF))
    return pl.pallas_call(
        kernel,
        out_shape=shapes,
        in_specs=[anywhere, anywhere, anywhere, anywhere, smem, smem, anywhere],
        out_specs=(anywhere, anywhere),
        scratch_shapes=[
            pltpu.VMEM((D, FF), BF),
            pltpu.VMEM((FF, D), BF),
            pltpu.VMEM((NODES, TOK, D), BF),
            pltpu.VMEM((QUAD, TILES, SUB, BLK), BF),
            pltpu.VMEM((5, 8, 128), jnp.int32),
            pltpu.VMEM((6, 8, 128), jnp.int32),
            pltpu.VMEM((QUAD * TILES * SUB, BLK), F32),
            pltpu.VMEM((BLOCKS * SUB, BLOCKS * BLK), BF),
            pltpu.VMEM((BLOCKS * SUB, BLOCKS * BLK), BF),
            pltpu.VMEM((NZ, NY, NC, CHUNKS, CN, D), BF),
            pltpu.VMEM((2, NX, D, 256), BF),
            pltpu.VMEM((NFC, NZ, 2, SUB, FC), F32),
            pltpu.VMEM((NFC, NZ, 2, SUB, FC), BF),
            pltpu.VMEM((NP, NZ, SUB, PW), BF),
            pltpu.VMEM((NP, NZ, SUB, PW), BF),
            pltpu.VMEM((NP, NZ, SUB, PW), BF),
            pltpu.VMEM((NZ, 2, SUB, PW), BF),
            pltpu.VMEM((SUB, PW), BF),
            pltpu.VMEM((SUB, PW), BF),
            pltpu.VMEM((NODES, D), BF),
            pltpu.VMEM((NODES, HID), BF),
            pltpu.VMEM((BLOCKS, BLK), F32),
            pltpu.VMEM((BLOCKS, BLK), F32),
            pltpu.VMEM((BLOCKS, BLK), F32),
            pltpu.VMEM((NZ, BLOCKS, BLK), F32),
            dma((17,)),
            dma((1,)), dma((1,)),
            dma((1,)), dma((1,)),
            dma((7,)), dma((7,)),
            dma((6, CHUNKS)), dma((6, CHUNKS)),
            dma((NP,)), dma((NP,)),
            dma((NP,)), dma((NP,)),
            dma((2,)), dma((2,)),
        ],
        compiler_params=pltpu.CompilerParams(
            collective_id=0, has_side_effects=True, vmem_limit_bytes=58 * 2**20
        ),
        cost_estimate=pl.CostEstimate(flops=12_000_000_000, bytes_accessed=16_000_000, transcendentals=3_200_000),
        name="encode_and_aggregate",
    )(tokens, w_in, w_out, tile_weights, tile_src, tile_dst, w_sage)


def solution(mesh):
    return jax.shard_map(
        on_device,
        mesh=mesh,
        in_specs=(
            P(("dp", "graph"), None, None),
            P(),
            P(),
            P(("dp", "graph"), None, None),
            P(("dp", "graph")),
            P(("dp", "graph")),
            P(None, "dp"),
        ),
        out_specs=(P(("dp", "graph"), None), P(("dp", "graph"), None)),
        check_vma=False,
    )
```

```python
import functools

import jax
import jax.numpy as jnp
from jax import lax
from jax.experimental import pallas as pl
from jax.experimental.pallas import tpu as pltpu
from jax.sharding import PartitionSpec as P

EPS = 1e-05
MESH = pl.DeviceIdType.MESH

NX, NZ, NY, NC = 4, 8, 4, 2
D, FF, HID = 768, 3072, 1024
BLK, TILES, BLOCKS = 128, 32, 16
NODES, TOK = 32, 32
CHUNKS = 4
CN = NODES // CHUNKS
ROWS = CN * TOK
FB = 768
NFB = FF // FB
QUAD = 4
SUB = BLK // QUAD
FC = 256
NFC = D // FC
PW = FC // 2
NP = D // PW
FIRST_Z = 1
POLL = (0, 2, 1, 3, 4, 5)
UNROLL = 8
ZORDER = (4, 3, 5, 2, 6, 1, 7)
YORDER = (2, 1, 3)
BF, F32 = jnp.bfloat16, jnp.float32


def kernel(
    tok_ref, win_ref, wout_ref, tw_ref, src_ref, dst_ref, ws_ref,
    emb_out, node_out,
    win, wout, tok, tiles, ids, ids_out, spread, adj, adj_t, emb, wg, own, out_y, in_y, out_z, in_z,
    in_z0, out_p, in_p, emb_v, node_v,
    deg, deg_in, deg_sum, deg_all,
    load_sem, tile_s, tile_r, id_s, id_r, w_s, w_r, ag_s, ag_r,
    vy_s, vy_r, vz_s, vz_r, d_s, d_r,
):
    xi = lax.axis_index("dp")
    g = lax.axis_index("graph")
    z, y, c = g // 8, (g // 2) % 4, g % 2
    q = g % 4
    yh = y // 2

    def at(zz, yy, cc):
        return (xi, (zz * NY + yy) * NC + cc)

    def zoff(j):
        return lax.rem(z + j + NZ, NZ)

    def yoff(j):
        return lax.rem(y + j + NY, NY)

    def xoff(j):
        return lax.rem(xi + j + NX, NX)

    def remote(src, dst, ss, rs, dev):
        return pltpu.make_async_remote_copy(
            src_ref=src, dst_ref=dst, send_sem=ss, recv_sem=rs, device_id=dev, device_id_type=MESH
        )

    sib = at(z, y, 1 - c)
    def load_tok(k):
        return pltpu.make_async_copy(tok_ref.at[pl.ds(k * CN, CN)], tok.at[pl.ds(k * CN, CN)], load_sem.at[k])

    def load_in(j):
        cols = pl.ds(j * FB, FB)
        return pltpu.make_async_copy(win_ref.at[:, cols], win.at[:, cols], load_sem.at[4 + j])

    def load_out(j):
        rows = pl.ds(j * FB, FB)
        return pltpu.make_async_copy(wout_ref.at[rows], wout.at[rows], load_sem.at[8 + j])

    def load_tiles():
        return pltpu.make_async_copy(
            tw_ref.at[:, pl.ds(pl.multiple_of(q * SUB, SUB), SUB)], tiles.at[0], load_sem.at[12]
        )

    def load_ws(h):
        return pltpu.make_async_copy(ws_ref.at[pl.ds(h * D, D)], wg.at[h, xi], load_sem.at[13 + h])

    peers = [at(zoff(j), y, c) for j in range(1, NZ)]
    peers += [at(z, yoff(j), c) for j in range(1, NY)]
    peers += [sib, at(z, yoff(1), 1 - c), at(z, yoff(-1), 1 - c), (xoff(1), g), (xoff(-1), g)]
    barrier = pltpu.get_barrier_semaphore()
    for dev in peers:
        pl.semaphore_signal(barrier, inc=1, device_id=dev, device_id_type=MESH)

    load_tok(0).start()
    for j in range(NFB):
        load_in(j).start()
        load_out(j).start()
    for k in range(1, CHUNKS):
        load_tok(k).start()
    load_tiles().start()
    for h in range(2):
        load_ws(h).start()

    low, high = (0, TILES // 2), (TILES // 2, TILES)
    share = [
        (sib, 1, (0, TILES)),
        (at(z, yoff(1), c), 2, low), (at(z, yoff(-1), c), 2, high),
        (at(z, yoff(1), 1 - c), 3, low), (at(z, yoff(-1), 1 - c), 3, high),
    ]

    lane = lax.broadcasted_iota(jnp.int32, (8, 128), 1)
    mine = jnp.full((8, 128), -1, jnp.int32)
    for t in range(TILES):
        mine = jnp.where(lax.rem(lane, TILES) == t, src_ref[t] * BLOCKS + dst_ref[t], mine)
    for n, (slot, (t0, t1)) in enumerate([(0, (0, TILES))] + [e[1:] for e in share]):
        ids_out[n] = jnp.where((lane >= slot * TILES + t0) & (lane < slot * TILES + t1), mine, -1)

    def tile_send(n):
        dev, slot, (t0, t1) = share[n]
        dq = (1 - c if n in (0, 3, 4) else c) + 2 * ((y % 2) if n == 0 else 1 - y % 2)
        part = pl.ds(t0, t1 - t0)
        return remote(tw_ref.at[part, pl.ds(pl.multiple_of(dq * SUB, SUB), SUB)], tiles.at[slot, part],
                      tile_s.at[0], tile_r.at[0], dev)

    def tile_all():
        slot = tiles.at[pl.ds(1, 3)]
        return remote(slot, slot, tile_s.at[0], tile_r.at[0], sib)

    def id_send(n):
        return remote(ids_out.at[n + 1], ids.at[n], id_s.at[0], id_r.at[0], share[n][0])

    def id_all():
        return remote(ids, ids, id_s.at[0], id_r.at[0], sib)

    half = pl.ds(pl.multiple_of(c * D, D), D)

    def w_send(n):
        return remote(ws_ref.at[half], wg.at[c, xi], w_s.at[n], w_r.at[n], (xoff(1 - 2 * n), g))

    def w_recv(n):
        slot = wg.at[c, xoff(2 * n - 1)]
        return remote(slot, slot, w_s.at[n], w_r.at[n], (xoff(1 - 2 * n), g))

    def w_fwd(n):
        rows = pl.ds(n * (D // 2), D // 2)
        slot = wg.at[c, xoff(2 * n - 1), rows]
        return remote(slot, slot, w_s.at[2 + n], w_r.at[2 + n], (xoff(1 - 2 * n), g))

    def w_fwd_recv(n):
        rows = pl.ds(n * (D // 2), D // 2)
        slot = wg.at[c, xoff(2), rows]
        return remote(slot, slot, w_s.at[2 + n], w_r.at[2 + n], (xoff(1 - 2 * n), g))

    def w_sib(n):
        slot = wg.at[c, xoff(n)]
        return remote(slot, slot, w_s.at[3 + n], w_r.at[3 + n], sib)

    def w_sib_recv(n):
        slot = wg.at[1 - c, xoff(n)]
        return remote(slot, slot, w_s.at[3 + n], w_r.at[3 + n], sib)

    def meet():
        pl.semaphore_wait(barrier, len(peers))
        for n in range(len(share)):
            id_send(n).start()
            tile_send(n).start()
        for n in range(2):
            w_send(n).start()

    def z1(k, j=None):
        slot = emb.at[pl.ds(0, NZ - 1) if j is None else z, y, c, k]
        return remote(slot, slot, ag_s.at[0, k], ag_r.at[0, k], at(zoff(j or 1), y, c))

    def ya(k, n, got=False):
        slot = emb.at[:, yoff(2 * n - 1) if got else y, c, k]
        return remote(slot, slot, ag_s.at[1 + n, k], ag_r.at[1 + n, k], at(z, yoff(1 - 2 * n), c))

    def yb(k, n, got=False):
        slot = emb.at[pl.ds(n * (NZ // 2), NZ // 2), yoff(2 if got else 2 * n - 1), c, k]
        return remote(slot, slot, ag_s.at[3 + n, k], ag_r.at[3 + n, k], at(z, yoff(1 - 2 * n), c))

    end = CHUNKS - 1
    front, back = pl.ds(0, D // 2), pl.ds(D // 2, D // 2)

    def zy1(j=None):
        slot = emb.at[pl.ds(0, NZ - 1) if j is None else z, y, c, end, :, front]
        return remote(slot, slot, ag_s.at[0, end], ag_r.at[0, end], at(zoff(j or 1), y, c))

    def zy2(j=None):
        slot = emb.at[:, pl.ds(0, NY - 1) if j is None else y, c, end, :, front]
        return remote(slot, slot, ag_s.at[1, end], ag_r.at[1, end], at(z, yoff(j or 1), c))

    def yz1(j=None):
        slot = emb.at[z, pl.ds(0, NY - 1) if j is None else y, c, end, :, back]
        return remote(slot, slot, ag_s.at[2, end], ag_r.at[2, end], at(z, yoff(j or 1), c))

    def yz2(j=None):
        slot = emb.at[pl.ds(0, NZ - 1) if j is None else z, :, c, end, :, back]
        return remote(slot, slot, ag_s.at[3, end], ag_r.at[3, end], at(zoff(j or 1), y, c))

    def c_send(k):
        slot = emb.at[:, :, c, k]
        return remote(slot, slot, ag_s.at[5, k], ag_r.at[5, k], sib)

    def c_recv(k):
        slot = emb.at[:, :, 1 - c, k]
        return remote(slot, slot, ag_s.at[5, k], ag_r.at[5, k], sib)

    def go_a(k, last=False):
        if last:
            for j in YORDER:
                yz1(j).start()
            for j in ZORDER:
                zy1(j).start()
            return
        for j in ZORDER:
            z1(k, j).start()

    def go_b(k):
        z1(k).wait_recv()
        for n in range(2):
            ya(k, n).start()

    def go_d(k):
        for n in range(2):
            ya(k, n, True).wait_recv()
            yb(k, n).start()

    def go_e():
        yz1().wait_recv()
        for j in ZORDER:
            yz2(j).start()

    def go_f():
        zy1().wait_recv()
        for j in YORDER:
            zy2(j).start()

    def go_c(k):
        if k < end:
            for n in range(2):
                yb(k, n, True).wait_recv()
        else:
            zy2().wait_recv()
            yz2().wait_recv()
        c_send(k).start()

    def left(k):
        if k < end:
            z1(k).wait_send()
            for n in range(2):
                ya(k, n).wait_send()
                yb(k, n).wait_send()
        else:
            for copies in (zy1, zy2, yz1, yz2):
                copies().wait_send()
        c_send(k).wait_send()

    def encode(k, carry, head=False, last=False):
        load_tok(k).wait()
        x = tok[pl.ds(k * CN, CN)].reshape(ROWS, D)
        acc = x.astype(F32)
        for j in range(NFB):
            if head:
                load_in(j).wait()
                load_out(j).wait()
            h = jnp.dot(x, win[:, j * FB:(j + 1) * FB], preferred_element_type=F32)
            a = (h * 0.5 * (1.0 + lax.erf(h * 0.7071067811865476))).astype(BF)
            acc = acc + jnp.dot(a, wout[j * FB:(j + 1) * FB, :], preferred_element_type=F32)
            if j == 1 and head:
                meet()
            if j == 1 and last:
                go_b(k - 2)
            elif j == 1 and not head:
                @pl.when(k >= 2)
                def _():
                    go_b(k - 2)
        cent = acc - jnp.mean(acc, axis=1, keepdims=True)
        var = jnp.mean(cent * cent, axis=1, keepdims=True)
        norm = cent * lax.rsqrt(var + EPS)
        emb[z, y, c, k] = jnp.mean(norm.reshape(CN, TOK, D), axis=1).astype(BF)

        go_a(k, last)
        return carry

    encode(0, 0, head=True)
    lax.fori_loop(1, end, encode, 0)
    encode(end, 0, last=True)
    for n in range(2):
        w_recv(n).wait_recv()
        w_fwd(n).start()
    go_d(0)
    go_b(2)

    load_tiles().wait()
    id_all().wait_recv()
    tile_all().wait_recv()
    for n in range(QUAD):
        spread[pl.ds(n * TILES * SUB, TILES * SUB), :] = tiles[n].astype(F32).reshape(TILES * SUB, BLK)
    cell = jnp.maximum(jnp.max(ids[...], axis=0), ids_out[0])[0:1, :]
    pick = (lax.broadcasted_iota(jnp.int32, (BLOCKS * BLOCKS, QUAD * TILES), 0) == cell).astype(BF)
    dlane = lax.broadcasted_iota(jnp.int32, (BLOCKS, BLK), 1)

    def place(n, found):
        for u in range(UNROLL):
            i = n * UNROLL + u
            rows = spread[pl.ds(i, QUAD * TILES, stride=SUB), :].astype(BF)
            got = jnp.dot(pick, rows, preferred_element_type=F32)
            total = got[:BLOCKS]
            to = pl.ds(pl.multiple_of(i * BLOCKS, BLOCKS), BLOCKS)
            for s in range(BLOCKS):
                part = got[s * BLOCKS:(s + 1) * BLOCKS]
                if s:
                    total = total + part
                adj[to, s * BLK:(s + 1) * BLK] = part.astype(BF)
            found = found + jnp.where(dlane == i, jnp.sum(total, axis=1, keepdims=True), 0.0)
        return found

    steps = SUB // UNROLL
    found = lax.fori_loop(0, steps // 2, place, jnp.zeros((BLOCKS, BLK), F32))
    go_d(1)
    go_e()
    deg[...] = lax.fori_loop(steps // 2, steps, place, found)

    partner = at(z, yoff(2), c)
    d_first = remote(deg, deg_in, d_s.at[0], d_r.at[0], partner)
    d_first.start()
    go_f()
    go_c(0)
    wide = BLOCKS * SUB
    r = lax.broadcasted_iota(jnp.int32, (wide, 1), 0)
    col = lax.broadcasted_iota(jnp.int32, (1, wide), 1)
    turn = (col == lax.rem(r, SUB) * BLOCKS + r // SUB).astype(BF)
    place_of = lax.rem(col, BLK) // NODES * BLK + lax.rem(col, NODES) // CN * NODES + col // BLK * CN + lax.rem(col, CN)
    turn_cols = (r == place_of).astype(BF)
    for n in range(4):
        cols = slice(n * wide, (n + 1) * wide)
        turned = jnp.dot(turn, adj[:, cols], preferred_element_type=F32).astype(BF)
        adj_t[:, cols] = jnp.dot(turned, turn_cols, preferred_element_type=F32).astype(BF)
        if n == 1:
            go_d(2)
            go_c(1)
    emb_v[...] = emb[z, y, c].astype(F32).reshape(NODES, D).astype(BF)
    save_emb = pltpu.make_async_copy(emb_v, emb_out, load_sem.at[15])
    save_emb.start()
    for n in range(2):
        w_fwd_recv(n).wait_recv()
    for n in range(1, 4):
        w_sib(n).start()
    d_first.wait_recv()
    deg_sum[...] = deg[...] + deg_in[...]

    def d_send(j):
        return remote(deg_sum, deg_all.at[j], d_s.at[1], d_r.at[1], at(zoff(j), y, c))

    def d_all():
        slot = deg_all.at[pl.ds(1, NZ - 1)]
        return remote(slot, slot, d_s.at[1], d_r.at[1], sib)

    for j in range(1, NZ):
        d_send(j).start()

    def weighted(chunks, f):
        left_side = [
            adj_t[:, n * wide + k * BLK:n * wide + (k + 1) * BLK] for k in chunks for n in range(4)
        ]
        right_side = [
            emb[:, :, :, k, :, f * FC:(f + 1) * FC].astype(F32).reshape(wide, FC).astype(BF) for k in chunks
        ]
        return jnp.dot(
            jnp.concatenate(left_side, axis=1), jnp.concatenate(right_side, axis=0), preferred_element_type=F32
        ).reshape(NZ, 2, SUB, FC)

    go_c(2)
    go_c(3)
    for k in range(2):
        c_recv(k).wait_recv()
    for f in range(NFC):
        own[f] = weighted((0, 1), f)
    for k in range(2, CHUNKS):
        c_recv(k).wait_recv()

    def lanes(p):
        return pl.ds(p % 2 * PW, PW)

    def vy(p):
        if p == FIRST_Z:
            src, dst = out_p, in_p
        else:
            src, dst = out_y.at[p // 2, :, 1 - yh, :, lanes(p)], in_y.at[p]
        return remote(src, dst, vy_s.at[p], vy_r.at[p], partner)

    def vz(p, j):
        if p == FIRST_Z:
            src, dst = out_y.at[p // 2, zoff(j), :, :, lanes(p)], in_z0.at[j]
        else:
            src, dst = out_z.at[p, zoff(j)], in_z.at[p, j]
        return remote(src, dst, vz_s.at[p], vz_r.at[p], at(zoff(j), y, c))

    def vz_all(p):
        slot = in_z0.at[pl.ds(1, NZ - 1)] if p == FIRST_Z else in_z.at[p, pl.ds(1, NZ - 1)]
        return remote(slot, slot, vz_s.at[p], vz_r.at[p], sib)

    def go_vz(p):
        if p == FIRST_Z:
            vz_all(p).wait_recv()
            for h in range(2):
                total = own[p // 2, z, h, :, lanes(p)]
                for j in range(1, NZ):
                    total = total + in_z0[j, h].astype(F32)
                own[p // 2, z, h, :, lanes(p)] = total
            out_p[...] = own[p // 2, z, 1 - yh, :, lanes(p)].astype(BF)
            vy(p).start()
            return
        vy(p).wait_recv()
        both = own[p // 2, :, yh, :, lanes(p)] + in_y[p].astype(F32)
        own[p // 2, :, yh, :, lanes(p)] = both
        out_z[p] = both.astype(BF)
        for j in ZORDER:
            vz(p, j).start()

    for f in range(NFC):
        v = own[f] + weighted((2, 3), f)
        own[f] = v
        out_y[f] = v.astype(BF)
        for p in (2 * f, 2 * f + 1):
            if p == FIRST_Z:
                for j in ZORDER:
                    vz(p, j).start()
            else:
                vy(p).start()
    id_all().wait_send()
    tile_all().wait_send()
    for n in range(2):
        w_send(n).wait_send()
        w_fwd(n).wait_send()
    for n in range(1, 4):
        w_sib(n).wait_send()

    for k in range(CHUNKS):
        left(k)
    d_first.wait_send()
    d_all().wait_send()

    for h in range(2):
        load_ws(h).wait()
    for n in range(1, 4):
        w_sib_recv(n).wait_recv()
    mine_emb = emb_v[...]
    pre = [jnp.dot(mine_emb, wg[0, n], preferred_element_type=F32) for n in range(NX)]

    for p in POLL:
        go_vz(p)

    degree = deg_sum[...]
    d_all().wait_recv()
    for j in range(1, NZ):
        degree = degree + deg_all[j]
    block = g // 4
    degree = jnp.sum(
        jnp.where(lax.broadcasted_iota(jnp.int32, (BLOCKS, BLK), 0) == block, degree, 0.0), axis=0, keepdims=True
    )
    on = lax.broadcasted_iota(jnp.int32, (NODES, BLK), 0) == lax.broadcasted_iota(jnp.int32, (NODES, BLK), 1)
    column = jnp.sum(jnp.where(on, jnp.broadcast_to(degree, (NODES, BLK)), 0.0), axis=1, keepdims=True)
    scale = lax.rsqrt(1.0 + column)

    for f in range(NFC):
        sides = []
        for p in (2 * f, 2 * f + 1):
            total = own[f, z, yh, :, lanes(p)]
            if p == FIRST_Z:
                vy(p).wait_recv()
                total = total + in_p[...].astype(F32)
            else:
                vz_all(p).wait_recv()
                for j in range(1, NZ):
                    total = total + in_z[p, j].astype(F32)
            sides.append((total * scale).astype(BF))
        agg = jnp.concatenate(sides, axis=1)
        for n in range(NX):
            pre[n] = pre[n] + jnp.dot(agg, wg[1, n, f * FC:(f + 1) * FC, :], preferred_element_type=F32)
    act = [jnp.maximum(p, 0.0) for p in pre]
    square = sum(jnp.sum(r * r, axis=1, keepdims=True) for r in act)
    inv = lax.rsqrt(square * (1.0 / HID) + EPS)
    for n in range(NX):
        node_v[:, n * 256:(n + 1) * 256] = (act[n] * inv).astype(BF)
    save_node = pltpu.make_async_copy(node_v, node_out, load_sem.at[16])
    save_node.start()

    save_emb.wait()
    save_node.wait()
    for p in range(NP):
        vy(p).wait_send()
        vz_all(p).wait_send()


def on_device(tokens, w_in, w_out, tile_weights, tile_src, tile_dst, w_sage):
    dma = pltpu.SemaphoreType.DMA
    anywhere = pl.BlockSpec(memory_space=pl.ANY)
    smem = pl.BlockSpec(memory_space=pltpu.SMEM)
    shapes = (jax.ShapeDtypeStruct((NODES, D), BF), jax.ShapeDtypeStruct((NODES, HID), BF))
    return pl.pallas_call(
        kernel,
        out_shape=shapes,
        in_specs=[anywhere, anywhere, anywhere, anywhere, smem, smem, anywhere],
        out_specs=(anywhere, anywhere),
        scratch_shapes=[
            pltpu.VMEM((D, FF), BF),
            pltpu.VMEM((FF, D), BF),
            pltpu.VMEM((NODES, TOK, D), BF),
            pltpu.VMEM((QUAD, TILES, SUB, BLK), BF),
            pltpu.VMEM((5, 8, 128), jnp.int32),
            pltpu.VMEM((6, 8, 128), jnp.int32),
            pltpu.VMEM((QUAD * TILES * SUB, BLK), F32),
            pltpu.VMEM((BLOCKS * SUB, BLOCKS * BLK), BF),
            pltpu.VMEM((BLOCKS * SUB, BLOCKS * BLK), BF),
            pltpu.VMEM((NZ, NY, NC, CHUNKS, CN, D), BF),
            pltpu.VMEM((2, NX, D, 256), BF),
            pltpu.VMEM((NFC, NZ, 2, SUB, FC), F32),
            pltpu.VMEM((NFC, NZ, 2, SUB, FC), BF),
            pltpu.VMEM((NP, NZ, SUB, PW), BF),
            pltpu.VMEM((NP, NZ, SUB, PW), BF),
            pltpu.VMEM((NP, NZ, SUB, PW), BF),
            pltpu.VMEM((NZ, 2, SUB, PW), BF),
            pltpu.VMEM((SUB, PW), BF),
            pltpu.VMEM((SUB, PW), BF),
            pltpu.VMEM((NODES, D), BF),
            pltpu.VMEM((NODES, HID), BF),
            pltpu.VMEM((BLOCKS, BLK), F32),
            pltpu.VMEM((BLOCKS, BLK), F32),
            pltpu.VMEM((BLOCKS, BLK), F32),
            pltpu.VMEM((NZ, BLOCKS, BLK), F32),
            dma((17,)),
            dma((1,)), dma((1,)),
            dma((1,)), dma((1,)),
            dma((7,)), dma((7,)),
            dma((6, CHUNKS)), dma((6, CHUNKS)),
            dma((NP,)), dma((NP,)),
            dma((NP,)), dma((NP,)),
            dma((2,)), dma((2,)),
        ],
        compiler_params=pltpu.CompilerParams(
            collective_id=0, has_side_effects=True, vmem_limit_bytes=58 * 2**20
        ),
        cost_estimate=pl.CostEstimate(flops=12_000_000_000, bytes_accessed=16_000_000, transcendentals=3_200_000),
        name="encode_and_aggregate",
    )(tokens, w_in, w_out, tile_weights, tile_src, tile_dst, w_sage)


def solution(mesh):
    return jax.shard_map(
        on_device,
        mesh=mesh,
        in_specs=(
            P(("dp", "graph"), None, None),
            P(),
            P(),
            P(("dp", "graph"), None, None),
            P(("dp", "graph")),
            P(("dp", "graph")),
            P(None, "dp"),
        ),
        out_specs=(P(("dp", "graph"), None), P(("dp", "graph"), None)),
        check_vma=False,
    )
```
